256 devices in a mesh: layer: 16 (over z, core), tensor: 16 (over y, x).
Axes of the slice: x: 4, y: 4, z: 8, core: 2. Of those that a mesh axis runs over, the one named last changes fastest.
Arguments:
- layer_input: bfloat16 [2, 128, 4096], P(None, None, 'tensor'), may hold values from -6 to 6
- weight: bfloat16 [16, 4096, 4096], P('layer', None, 'tensor'), may hold values from -0.09375 to 0.09375
- gain: bfloat16 [16, 4096], P('layer'), may hold values from 0.099609375 to 1.8984375
- block_mask: int32 [16, 32, 32], P('layer', None, 'tensor'), may hold values 0 or 1
Outputs:
- kept_grad: float32 [16, 4096, 4096], P('layer', None, 'tensor')
- recon_loss: float32 [16], P('layer')
The draws below stay inside these ranges and needn't reach their ends.
Inputs may be any that keep to these rules, and one draw needn't show every extreme that they name: `block_mask`: 1 keeps a 128 x 128 block of weights, 0 prunes it.
All inputs are finite; a program needn't handle non-finite values.
Results may differ from the reference program's by a relative error of at most 0.029.
Values may be sent and summed in bfloat16 or wider, within the bound.
No kernel may reach another device: no remote copies, remote signals or barrier semaphores. Data moves between devices by JAX's collectives and lax.ppermute only.
A program may use at most 64 MiB of HBM per device.

```python
import jax
import jax.numpy as jnp
from jax import lax

D = 4096
BLOCK = 128
ROWS = 128
MICRO = 2
LAYERS = 16
DB = 32


def with_ends(values, stream_key, smallest, top_value):
    longest = values.shape.index(max(values.shape))
    spots = []
    for shift in (0, 1):
        where = [jax.random.randint(jax.random.fold_in(stream_key, axis), (), 0, length) for axis, length in enumerate(values.shape)]
        where[longest] = (where[longest] + shift) % values.shape[longest]
        spots.append(tuple(where))
    return values.at[spots[0]].set(smallest).at[spots[1]].set(top_value)


def steps_of(own_key, dims, shards, smallest, high):
    level = 1.0
    for position, shards_of in shards:
        draws = jax.random.uniform(jax.random.fold_in(jax.random.fold_in(own_key, 6), position), (shards_of,), jnp.float32, smallest / len(shards), high / len(shards))
        level = level * jnp.repeat(jnp.exp(draws), dims[position] // shards_of).reshape((-1,) + (1,) * (len(dims) - 1 - position))
    return level


def bell_draw(key, shape, deviation, reach, pieces=(), held_as=jnp.bfloat16):
    factor_of = steps_of(key, shape, pieces, -0.22, 0.18) if pieces else 1.0
    drawn = jax.random.normal(key, shape, jnp.float32) * deviation * factor_of
    return jnp.minimum(jnp.maximum(drawn, -reach), reach).astype(held_as)


def setup_inputs(seed: int = 0) -> dict:
    seeds = jax.random.split(jax.random.key(seed), 5)
    layer_input = bell_draw(seeds[0], (MICRO, ROWS, D), 1.0, 6.0, ((2, 16),))
    weight = bell_draw(seeds[1], (LAYERS, D, D), D ** -0.5, 0.09375, ((0, 16), (2, 16)))
    gain = jnp.clip(1.0 + 0.18 * jax.random.normal(seeds[2], (LAYERS, D), jnp.float32), 0.099609375, 1.8984375).astype(jnp.bfloat16)
    block_mask = with_ends((jax.random.randint(seeds[3], (LAYERS, DB, DB), 0, 2) < 1).astype(jnp.int32), jax.random.fold_in(seeds[3], 1), 0, 1)
    return {"layer_input": layer_input, "weight": weight, "gain": gain, "block_mask": block_mask}


epsilon = 1e-05

def reference(layer_input, weight, gain, block_mask):
    current = layer_input.reshape(MICRO * ROWS, D)
    grad_list = []
    loss_list = []
    for layer_index in range(LAYERS):
        values = current.astype(jnp.float32)
        inv_rms = lax.rsqrt(lax.optimization_barrier(jnp.mean(values * values, axis=-1, keepdims=True)) + epsilon)
        normed = (values * inv_rms * gain[layer_index].astype(jnp.float32)).astype(jnp.bfloat16)
        keep_mask = jnp.repeat(jnp.repeat(block_mask[layer_index], BLOCK, axis=0), BLOCK, axis=1).astype(jnp.bfloat16)
        teacher = jnp.dot(normed, weight[layer_index], preferred_element_type=jnp.float32)
        student = jnp.dot(normed, weight[layer_index] * keep_mask, preferred_element_type=jnp.float32)
        error_rows = student - teacher
        error_bf = error_rows.astype(jnp.bfloat16)
        grad_full = lax.dot_general(normed, error_bf, (((0,), (0,)), ((), ())), preferred_element_type=jnp.float32) / ROWS
        grad_list.append(grad_full * keep_mask.astype(jnp.float32))
        loss_list.append(jnp.sum(error_rows * error_rows) / (ROWS * D))
        current = (values + teacher).astype(jnp.bfloat16)
    return (jnp.stack(grad_list), jnp.stack(loss_list))
```

```python
import jax
import jax.numpy as jnp
from jax import lax
from jax.experimental import pallas as pl
from jax.experimental.pallas import tpu as pltpu
from jax.sharding import PartitionSpec as P

BLOCK = 128
EPSILON = 1e-05
AXES = ("layer", "tensor")


def vmem():
    return pl.BlockSpec(memory_space=pltpu.VMEM)


def smem():
    return pl.BlockSpec(memory_space=pltpu.SMEM)


def hbm():
    return pl.BlockSpec(memory_space=pl.ANY)


def chain_kernel(place, own, blocks, gain, weights, kept_in, out, kept, sem):
    count, rows, width = blocks.shape
    save = pltpu.make_async_copy(blocks, kept.at[place[1]], sem)

    @pl.when(place[0] == 1)
    def _():
        save.start()

    squares = jnp.zeros((rows, width), jnp.float32)
    total = jnp.zeros((rows, weights.shape[1]), jnp.float32)
    for s in range(count):
        x = blocks[s].astype(jnp.float32)
        squares = squares + x * x
        scaled = (x * gain[s : s + 1, :].astype(jnp.float32)).astype(jnp.bfloat16)
        total = total + jnp.dot(
            scaled, weights[s * width : (s + 1) * width, :], preferred_element_type=jnp.float32
        )
    mean = jnp.sum(squares, axis=1, keepdims=True) / (count * width)
    new = (own[...].astype(jnp.float32) + lax.rsqrt(mean + EPSILON) * total).astype(jnp.bfloat16)
    for s in range(out.shape[0]):
        out[s] = new

    @pl.when(place[0] == 1)
    def _():
        save.wait()


def chain_layer(place, own, blocks, gain, weights, kept):
    return pl.pallas_call(
        chain_kernel,
        out_shape=(
            jax.ShapeDtypeStruct(blocks.shape, jnp.bfloat16),
            jax.ShapeDtypeStruct(kept.shape, kept.dtype),
        ),
        in_specs=[smem(), vmem(), vmem(), vmem(), vmem(), hbm()],
        out_specs=(vmem(), hbm()),
        scratch_shapes=[pltpu.SemaphoreType.DMA],
        input_output_aliases={5: 1},
        compiler_params=pltpu.CompilerParams(vmem_limit_bytes=32 * 1024 * 1024),
        name="chain_layer",
    )(place, own, blocks, gain, weights, kept)


def save_kernel(place, blocks, kept_in, kept, sem):
    @pl.when(place[0] == 1)
    def _():
        save = pltpu.make_async_copy(blocks, kept.at[place[1]], sem)
        save.start()
        save.wait()


def save_rows(place, blocks, kept):
    return pl.pallas_call(
        save_kernel,
        out_shape=jax.ShapeDtypeStruct(kept.shape, kept.dtype),
        in_specs=[smem(), hbm(), hbm()],
        out_specs=hbm(),
        scratch_shapes=[pltpu.SemaphoreType.DMA],
        input_output_aliases={2: 0},
        name="save_rows",
    )(place, blocks, kept)


def error_kernel(first, second, gain, weights, keep, normed, error_bf, loss):
    count, rows, width = first.shape
    for half, source in enumerate((first, second)):
        span = slice(half * rows, (half + 1) * rows)
        squares = jnp.zeros((rows, width), jnp.float32)
        for s in range(count):
            x = source[s].astype(jnp.float32)
            squares = squares + x * x
        inv = lax.rsqrt(jnp.sum(squares, axis=1, keepdims=True) / (count * width) + EPSILON)
        for s in range(count):
            x = source[s].astype(jnp.float32)
            normed[s, span, :] = (x * inv * gain[s : s + 1, :].astype(jnp.float32)).astype(jnp.bfloat16)
    total = jnp.zeros((2 * rows, weights.shape[1]), jnp.float32)
    per = width // BLOCK
    for s in range(count):
        for b in range(per):
            i = s * per + b
            pruned = weights[i * BLOCK : (i + 1) * BLOCK, :] * (1 - keep[i : i + 1, :]).astype(jnp.bfloat16)
            total = total - jnp.dot(
                normed[s, :, b * BLOCK : (b + 1) * BLOCK], pruned, preferred_element_type=jnp.float32
            )
    error_bf[...] = total.astype(jnp.bfloat16)
    part = jnp.sum(total * total, axis=0, keepdims=True)
    part = part[:, :128] + part[:, 128:]
    loss[...] = jnp.broadcast_to(part, loss.shape)


def grad_kernel(normed, error_bf, keep, out):
    width = normed.shape[2]
    product = lax.dot_general(
        normed[0], error_bf[...], (((0,), (0,)), ((), ())), preferred_element_type=jnp.float32
    )
    for b in range(width // BLOCK):
        span = slice(b * BLOCK, (b + 1) * BLOCK)
        out[span, :] = product[span, :] * (1.0 / 128) * keep[0, b : b + 1, :]


def tail(first, second, gain, weights, keep, full_width, micro_rows):
    count, rows, width = first.shape
    cols = weights.shape[1]
    normed, error_bf, loss = pl.pallas_call(
        error_kernel,
        out_shape=(
            jax.ShapeDtypeStruct((count, 2 * rows, width), jnp.bfloat16),
            jax.ShapeDtypeStruct((2 * rows, cols), jnp.bfloat16),
            jax.ShapeDtypeStruct((8, 128), jnp.float32),
        ),
        in_specs=[vmem()] * 5,
        out_specs=(vmem(),) * 3,
        compiler_params=pltpu.CompilerParams(vmem_limit_bytes=32 * 1024 * 1024),
        name="layer_error",
    )(first, second, gain, weights, keep)
    grad = pl.pallas_call(
        grad_kernel,
        grid=(count,),
        out_shape=jax.ShapeDtypeStruct((count * width, cols), jnp.float32),
        in_specs=[
            pl.BlockSpec((1, 2 * rows, width), lambda s: (s, 0, 0)),
            pl.BlockSpec((2 * rows, cols), lambda s: (0, 0)),
            pl.BlockSpec((1, width // BLOCK, cols), lambda s: (s, 0, 0)),
        ],
        out_specs=pl.BlockSpec((width, cols), lambda s: (s, 0)),
        compiler_params=pltpu.CompilerParams(vmem_limit_bytes=32 * 1024 * 1024),
        name="layer_grad",
    )(normed, error_bf, keep.reshape(count, width // BLOCK, cols))
    shares = lax.all_to_all(jnp.broadcast_to(loss, (16, 8, 128)), "tensor", 0, 0)
    total = jnp.sum(shares[:, 0, :]) / (micro_rows * full_width)
    return grad, total


def shards(layer_input, weight, gain, block_mask):
    layers = lax.axis_size("layer")
    tensors = lax.axis_size("tensor")
    planes = layers // 2
    layer = lax.axis_index("layer")
    plane, core = layer // 2, layer % 2
    micro, rows, width = layer_input.shape
    weights = weight[0]
    full_width = weights.shape[0]
    everyone = [(l, t) for l in range(layers) for t in range(tensors)]
    swap = [(l * tensors + t, (l ^ 1) * tensors + t) for l, t in everyone]
    hop = [(l * tensors + t, ((l + 2) % layers) * tensors + t) for l, t in everyone]

    gains = gain[0].reshape(tensors, width)
    other_weights = lax.ppermute(weights, AXES, swap)
    other_gains = lax.ppermute(gains, AXES, swap)
    first = core == 0
    w = (jnp.where(first, weights, other_weights), jnp.where(first, other_weights, weights))
    g = (jnp.where(first, gains, other_gains), jnp.where(first, other_gains, gains))

    kept = jnp.zeros((2, tensors, rows, width), jnp.bfloat16)
    own = lax.dynamic_index_in_dim(layer_input, core, 0, keepdims=False)
    send = jnp.broadcast_to(own, (tensors, rows, width))
    for step in range(planes):
        for parity in (0, 1):
            place = jnp.stack(
                [(plane == step).astype(jnp.int32), (core != parity).astype(jnp.int32)]
            )
            if step and not parity:
                own = lax.ppermute(own, AXES, hop)
                send = jnp.broadcast_to(own, (tensors, rows, width))
            blocks = lax.all_to_all(send, "tensor", 0, 0)
            if step == planes - 1 and parity:
                kept = save_rows(place, blocks, kept)
            else:
                send, kept = chain_layer(place, own, blocks, g[parity], w[parity], kept)
                own = send[0]
    arrived = lax.ppermute(kept[1], AXES, swap)
    keep = jnp.repeat(block_mask[0].astype(jnp.float32), BLOCK, axis=1)
    grad, total = tail(kept[0], arrived, gains, weights, keep, full_width, rows)
    return grad[None], total.reshape(1)


def solution(mesh):
    in_specs = (
        P(None, None, "tensor"),
        P("layer", None, "tensor"),
        P("layer", None),
        P("layer", None, "tensor"),
    )
    out_specs = (P("layer", None, "tensor"), P("layer"))
    return jax.shard_map(shards, mesh=mesh, in_specs=in_specs, out_specs=out_specs, check_vma=False)
```

```python
import jax
import jax.numpy as jnp
from jax import lax
from jax.experimental import pallas as pl
from jax.experimental.pallas import tpu as pltpu
from jax.sharding import PartitionSpec as P

BLOCK = 128
EPSILON = 1e-05
AXES = ("layer", "tensor")
SIDE = 4
NEAR = ((0, 0), (0, 1), (0, 3), (0, 2))
GROUP = ((0, 0), (1, 0), (3, 0), (2, 0))
MIB = 1024 * 1024


def vmem():
    return pl.BlockSpec(memory_space=pltpu.VMEM)


def smem():
    return pl.BlockSpec(memory_space=pltpu.SMEM)


def hbm():
    return pl.BlockSpec(memory_space=pl.ANY)


def params(mib):
    return pltpu.CompilerParams(vmem_limit_bytes=mib * MIB)


def wide_kernel(place, x_hbm, gains, mine, other, *refs, receivers):
    if receivers:
        out, kept, x, w, new, x_sems, w_sems, out_sem, save_sem = refs
    else:
        out, kept, x, w, x_sems, w_sems, save_sem = refs
    count, rows, width = x.shape
    chunks = x_sems.shape[0]
    per = count // chunks
    row_set, me, swapped = (place[i] for i in range(3))

    def x_copy(i):
        span = pl.ds(i * per, per)
        return pltpu.make_async_copy(x_hbm.at[span], x.at[span], x_sems.at[i])

    def w_copy(i, source):
        span = pl.ds(i * per * width, per * width)
        return pltpu.make_async_copy(source.at[span], w.at[span], w_sems.at[i])

    for i in range(chunks):
        x_copy(i).start()

    @pl.when(swapped == 0)
    def _():
        for i in range(chunks):
            w_copy(i, mine).start()

    @pl.when(swapped == 1)
    def _():
        for i in range(chunks):
            w_copy(i, other).start()

    squares = jnp.zeros((rows, width), jnp.float32)
    total = jnp.zeros((rows, w.shape[1]), jnp.float32)
    for i in range(chunks):
        x_copy(i).wait()
        w_copy(i, mine).wait()
        for s in range(i * per, (i + 1) * per):
            v = x[s].astype(jnp.float32)
            squares = squares + v * v
            g = gains[swapped, s : s + 1, :].astype(jnp.float32)
            total = total + jnp.dot(
                (v * g).astype(jnp.bfloat16),
                w[s * width : (s + 1) * width, :],
                preferred_element_type=jnp.float32,
            )
    part = kept.shape[1]
    save = pltpu.make_async_copy(
        x.at[:, pl.ds(pl.multiple_of(row_set * part, part), part), :], kept, save_sem
    )
    save.start()
    mean = jnp.sum(squares, axis=1, keepdims=True) / (count * width)
    result = (x[me].astype(jnp.float32) + lax.rsqrt(mean + EPSILON) * total).astype(jnp.bfloat16)
    if receivers:
        new[...] = result
        for s in range(receivers):
            pltpu.make_async_copy(new, out.at[s], out_sem.at[s]).start()
        for s in range(receivers):
            pltpu.make_async_copy(new, out.at[s], out_sem.at[s]).wait()
    else:
        out[...] = result
    save.wait()


def wide_layer(place, x, gains, mine, other, part, receivers):
    count, rows, width = x.shape
    full, cols = mine.shape
    chunks = 4
    out = (receivers, rows, cols) if receivers else (rows, cols)
    dma = pltpu.SemaphoreType.DMA
    scratch = [pltpu.VMEM(x.shape, x.dtype), pltpu.VMEM(mine.shape, mine.dtype)]
    scratch += [pltpu.VMEM((rows, cols), x.dtype)] if receivers else []
    scratch += [dma((chunks,)), dma((chunks,))]
    scratch += [dma((receivers,))] if receivers else []
    scratch += [dma]

    def kernel(*refs):
        wide_kernel(*refs, receivers=receivers)

    return pl.pallas_call(
        kernel,
        out_shape=(
            jax.ShapeDtypeStruct(out, x.dtype),
            jax.ShapeDtypeStruct((count, part, width), x.dtype),
        ),
        in_specs=[smem(), hbm(), vmem(), hbm(), hbm()],
        out_specs=(hbm() if receivers else vmem(), hbm()),
        scratch_shapes=scratch,
        compiler_params=params(16),
        name="wide_layer",
    )(place, x, gains, mine, other)


def fetch_kernel(place, *refs, parts):
    count = len(parts)
    mine, other = refs[:count], refs[count : 2 * count]
    out, sems = refs[2 * count :]

    def copies(sources):
        for i, (slot, row, rows) in enumerate(parts):
            yield pltpu.make_async_copy(sources[i], out.at[slot, pl.ds(row, rows)], sems.at[i])

    @pl.when(place[2] == 0)
    def _():
        for copy in copies(mine):
            copy.start()

    @pl.when(place[2] == 1)
    def _():
        for copy in copies(other):
            copy.start()

    for copy in copies(mine):
        copy.wait()


def fetch(place, mine, other):
    full, cols = mine[0].shape
    parts, at = [], 0
    for part in mine:
        parts.append((at // full, at % full, part.shape[0]))
        at += part.shape[0]

    def kernel(*refs):
        fetch_kernel(*refs, parts=parts)

    return pl.pallas_call(
        kernel,
        out_shape=jax.ShapeDtypeStruct((at // full, full, cols), jnp.bfloat16),
        in_specs=[smem()] + [hbm()] * (2 * len(mine)),
        out_specs=vmem(),
        scratch_shapes=[pltpu.SemaphoreType.DMA((len(mine),))],
        compiler_params=params(24),
        cost_estimate=pl.CostEstimate(flops=0, bytes_accessed=at * cols * 2, transcendentals=0),
        name="fetch_weights",
    )(place, *mine, *other)


def group_kernel(place, table, *refs, pieces, near):
    got, refs = refs[:pieces], refs[pieces:]
    gains, w, new, x = refs
    count, rows, width = x.shape
    swapped = place[2]
    if pieces == 1:
        for s in range(count):
            x[s] = got[0][s]
    else:
        for k in range(pieces):
            for j in range(near):
                x[table[k * near + j]] = got[k][j]
    squares = jnp.zeros((rows, width), jnp.float32)
    scaled = []
    for s in range(count):
        v = x[s].astype(jnp.float32)
        squares = squares + v * v
        g = gains[swapped, s : s + 1, :].astype(jnp.float32)
        scaled.append((v * g).astype(jnp.bfloat16))
    scaled = jnp.concatenate(scaled, axis=1)
    inv = lax.rsqrt(jnp.sum(squares, axis=1, keepdims=True) / (count * width) + EPSILON)
    for j in range(near):
        total = jnp.dot(scaled, w[j], preferred_element_type=jnp.float32)
        new[j] = (x[table[j]].astype(jnp.float32) + inv * total).astype(jnp.bfloat16)


def group_layer(place, table, got, gains, w):
    near, full, cols = w.shape
    rows, width = got[0].shape[1:]
    count = full // width

    def kernel(*refs):
        group_kernel(*refs, pieces=len(got), near=near)

    return pl.pallas_call(
        kernel,
        out_shape=(
            jax.ShapeDtypeStruct((near, rows, cols), jnp.bfloat16),
            jax.ShapeDtypeStruct((count, rows, width), jnp.bfloat16),
        ),
        in_specs=[smem(), smem()] + [vmem()] * (len(got) + 2),
        out_specs=(vmem(), vmem()),
        compiler_params=params(24),
        name="group_layer",
    )(place, table, *got, gains, w)


def order_kernel(table, *refs):
    got, x = refs[:-1], refs[-1]
    near = got[0].shape[0]
    for k in range(len(got)):
        for j in range(near):
            x[table[k * near + j]] = got[k][j]


def order_rows(table, got):
    near, rows, width = got[0].shape
    return pl.pallas_call(
        order_kernel,
        out_shape=jax.ShapeDtypeStruct((len(got) * near, rows, width), jnp.bfloat16),
        in_specs=[smem()] + [vmem()] * len(got),
        out_specs=vmem(),
        name="order_rows",
    )(table, *got)


def unset(*shapes):
    def kernel(*refs):
        pass

    return pl.pallas_call(
        kernel,
        out_shape=tuple(jax.ShapeDtypeStruct(s, jnp.bfloat16) for s in shapes),
        out_specs=tuple(hbm() for _ in shapes),
        name="unset",
    )()


def error_kernel(*refs, sources):
    xs, refs = refs[:sources], refs[sources:]
    gain, weights, keep, normed, error_bf, loss = refs
    sets, count, rows, width = xs[0].shape
    span = 0
    for source in xs:
        for h in range(sets):
            squares = jnp.zeros((rows, width), jnp.float32)
            for s in range(count):
                x = source[h, s].astype(jnp.float32)
                squares = squares + x * x
            inv = lax.rsqrt(jnp.sum(squares, axis=1, keepdims=True) / (count * width) + EPSILON)
            for s in range(count):
                x = source[h, s].astype(jnp.float32)
                scaled = x * inv * gain[s : s + 1, :].astype(jnp.float32)
                normed[s, span : span + rows, :] = scaled.astype(jnp.bfloat16)
            span += rows
    total = jnp.zeros((span, weights.shape[1]), jnp.float32)
    per = width // BLOCK
    for s in range(count):
        for b in range(per):
            i = s * per + b
            pruned = weights[i * BLOCK : (i + 1) * BLOCK, :] * (1 - keep[i : i + 1, :]).astype(jnp.bfloat16)
            total = total - jnp.dot(
                normed[s, :, b * BLOCK : (b + 1) * BLOCK], pruned, preferred_element_type=jnp.float32
            )
    error_bf[...] = total.astype(jnp.bfloat16)
    part = jnp.sum(total * total, axis=0, keepdims=True)
    part = part[:, :128] + part[:, 128:]
    loss[...] = jnp.broadcast_to(part, loss.shape)


def grad_kernel(normed, error_bf, keep, out, *, rows):
    width = normed.shape[2]
    per = width // BLOCK
    for s in range(normed.shape[0]):
        product = lax.dot_general(
            normed[s], error_bf[...], (((0,), (0,)), ((), ())), preferred_element_type=jnp.float32
        )
        for b in range(per):
            span = slice(b * BLOCK, (b + 1) * BLOCK)
            out[s * width + b * BLOCK : s * width + (b + 1) * BLOCK, :] = (
                product[span, :] * (1.0 / rows) * keep[s, b : b + 1, :]
            )


def tail(xs, gain, weights, keep, full_width, micro_rows):
    sets, count, rows, width = xs[0].shape
    rows = rows * sets * len(xs)
    cols = weights.shape[1]

    def kernel(*refs):
        error_kernel(*refs, sources=len(xs))

    def grads(*refs):
        grad_kernel(*refs, rows=micro_rows)

    normed, error_bf, loss = pl.pallas_call(
        kernel,
        out_shape=(
            jax.ShapeDtypeStruct((count, rows, width), jnp.bfloat16),
            jax.ShapeDtypeStruct((rows, cols), jnp.bfloat16),
            jax.ShapeDtypeStruct((8, 128), jnp.float32),
        ),
        in_specs=[vmem()] * (len(xs) + 3),
        out_specs=(vmem(),) * 3,
        compiler_params=params(24),
        name="layer_error",
    )(*xs, gain, weights, keep)
    step = 4
    grad = pl.pallas_call(
        grads,
        grid=(count // step,),
        out_shape=jax.ShapeDtypeStruct((count * width, cols), jnp.float32),
        in_specs=[
            pl.BlockSpec((step, rows, width), lambda s: (s, 0, 0)),
            pl.BlockSpec((rows, cols), lambda s: (0, 0)),
            pl.BlockSpec((step, width // BLOCK, cols), lambda s: (s, 0, 0)),
        ],
        out_specs=pl.BlockSpec((step * width, cols), lambda s: (s, 0)),
        compiler_params=params(24),
        name="layer_grad",
    )(normed, error_bf, keep.reshape(count, width // BLOCK, cols))
    shares = lax.all_to_all(jnp.broadcast_to(loss, (16, 8, 128)), "tensor", 0, 0)
    total = jnp.sum(shares[:, 0, :]) / (micro_rows * full_width)
    return grad, total


def shards(layer_input, weight, gain, block_mask):
    layers = lax.axis_size("layer")
    tensors = lax.axis_size("tensor")
    planes = layers // 2
    layer = lax.axis_index("layer")
    me = lax.axis_index("tensor").astype(jnp.int32)
    plane, core = layer // 2, layer % 2
    my_x, my_y = me % SIDE, me // SIDE
    micro, rows, width = layer_input.shape
    weights = weight[0]
    full_width = weights.shape[0]
    group_rows = rows // SIDE
    kept_shape = (tensors, group_rows, width)
    half = full_width // 2

    def from_chip(value, shift):
        route = []
        for l in range(layers):
            for t in range(tensors):
                source = ((t // SIDE + shift[1]) % SIDE) * SIDE + (t % SIDE + shift[0]) % SIDE
                route.append((l * tensors + source, l * tensors + t))
        return lax.ppermute(value, AXES, route)

    def swap(value):
        route = [
            (l * tensors + t, (l ^ 1) * tensors + t) for l in range(layers) for t in range(tensors)
        ]
        return lax.ppermute(value, AXES, route)

    def hop(value, to):
        route = [
            ((l - 2) * tensors + t, l * tensors + t)
            for l in (2 * to, 2 * to + 1)
            for t in range(tensors)
        ]
        return lax.ppermute(value, AXES, route)

    table = jnp.stack(
        [((my_y + j[1]) % SIDE) * SIDE + (my_x + k[0]) % SIDE for k in GROUP for j in NEAR]
    )

    def place(parity):
        return jnp.stack([my_y, me, (core != parity).astype(jnp.int32)])

    places = (place(0), place(1))
    own_gains = gain[0].reshape(tensors, width)
    gains = jnp.stack([own_gains, swap(own_gains)])
    other_weights = swap(weights)

    def wide_plane(own):
        send = jnp.broadcast_to(own, (tensors, rows, width))
        x = lax.all_to_all(send, "tensor", 0, 0)
        send, kept0 = wide_layer(places[0], x, gains, weights, other_weights, group_rows, tensors)
        x = lax.all_to_all(send, "tensor", 0, 0)
        new, kept1 = wide_layer(places[1], x, gains, weights, other_weights, group_rows, 0)
        return new, kept0, kept1

    part_shapes = [(full_width, width)] * 2 + [(half, width)] * 2

    def first_planes():
        start = lax.dynamic_index_in_dim(layer_input, core, 0, keepdims=False)
        new, kept0, kept1 = lax.cond(
            plane == 0,
            lambda: wide_plane(start),
            lambda: tuple(unset(start.shape, kept_shape, kept_shape)),
        )
        new = hop(new, 1)
        new, kept0, kept1 = lax.cond(
            plane == 1, lambda: wide_plane(new), lambda: (new, kept0, kept1)
        )
        return (new, kept0, kept1) + tuple(unset(*part_shapes, *part_shapes))

    def collect_weights():
        up = from_chip(weights, (0, 1))
        down = from_chip(weights, (0, 3))
        far = (from_chip(up[:half], (0, 1)), from_chip(down[half:], (0, 3)))
        mine = (up, down) + far
        return tuple(unset((rows, width), kept_shape, kept_shape)) + mine + tuple(swap(m) for m in mine)

    new, kept0, kept1, *parts = lax.cond(plane < 2, first_planes, collect_weights)
    mine = [weights] + parts[:4]
    other = [other_weights] + parts[4:]
    new = new.reshape(SIDE, group_rows, width)

    def group_plane(step, new):
        if step == 2:
            send = jnp.repeat(new, SIDE, axis=0)
            got = [lax.all_to_all(send, "tensor", 0, 0)]
        else:
            got = [new] + [from_chip(new, k) for k in GROUP[1:]]
        w = fetch(places[0], mine, other)
        new, kept0 = group_layer(places[0], table, got, gains, w)
        got = [new] + [from_chip(new, k) for k in GROUP[1:]]
        if step == planes - 1:
            return new, kept0, order_rows(table, got)
        w = fetch(places[1], mine, other)
        new, kept1 = group_layer(places[1], table, got, gains, w)
        return new, kept0, kept1

    for step in range(2, planes):
        new = hop(new, step)
        new, kept0, kept1 = lax.cond(
            plane == step,
            lambda new=new, step=step: group_plane(step, new),
            lambda new=new, a=kept0, b=kept1: (new, a, b),
        )

    first = core == 0
    arrived = swap(jnp.where(first, kept1, kept0))
    both = jnp.stack([jnp.where(first, kept0, kept1), arrived])
    xs = [both] + [from_chip(both, j) for j in NEAR[1:]]
    keep = jnp.repeat(block_mask[0].astype(jnp.float32), BLOCK, axis=1)
    grad, total = tail(xs, own_gains, weights, keep, full_width, rows)
    return grad[None], total.reshape(1)


def solution(mesh):
    in_specs = (
        P(None, None, "tensor"),
        P("layer", None, "tensor"),
        P("layer", None),
        P("layer", None, "tensor"),
    )
    out_specs = (P("layer", None, "tensor"), P("layer"))
    return jax.shard_map(shards, mesh=mesh, in_specs=in_specs, out_specs=out_specs, check_vma=False)
```

```python
import jax
import jax.numpy as jnp
from jax import lax
from jax.experimental import pallas as pl
from jax.experimental.pallas import tpu as pltpu
from jax.sharding import PartitionSpec as P

BLOCK = 128
EPSILON = 1e-05
AXES = ("layer", "tensor")
SIDE = 4
NEAR = ((0, 0), (0, 1), (0, 3), (0, 2))
GROUP = ((0, 0), (1, 0), (3, 0), (2, 0))
MIB = 1024 * 1024


def vmem():
    return pl.BlockSpec(memory_space=pltpu.VMEM)


def smem():
    return pl.BlockSpec(memory_space=pltpu.SMEM)


def hbm():
    return pl.BlockSpec(memory_space=pl.ANY)


def params(mib):
    return pltpu.CompilerParams(vmem_limit_bytes=mib * MIB)


def wide_kernel(me, x_hbm, gain, w_hbm, *refs, receivers):
    if receivers:
        new, out, x, w, x_sems, w_sems, out_sems = refs
    else:
        new, x, w, x_sems, w_sems = refs
    count, rows, width = x.shape
    chunks = x_sems.shape[0]
    per = count // chunks

    def x_copy(i):
        span = pl.ds(i * per, per)
        return pltpu.make_async_copy(x_hbm.at[span], x.at[span], x_sems.at[i])

    def w_copy(i):
        span = pl.ds(i * per * width, per * width)
        return pltpu.make_async_copy(w_hbm.at[span], w.at[span], w_sems.at[i])

    for i in range(chunks):
        x_copy(i).start()
        w_copy(i).start()
    squares = jnp.zeros((rows, width), jnp.float32)
    total = jnp.zeros((rows, w.shape[1]), jnp.float32)
    for i in range(chunks):
        x_copy(i).wait()
        w_copy(i).wait()
        for s in range(i * per, (i + 1) * per):
            v = x[s].astype(jnp.float32)
            squares = squares + v * v
            g = gain[s : s + 1, :].astype(jnp.float32)
            total = total + jnp.dot(
                (v * g).astype(jnp.bfloat16),
                w[s * width : (s + 1) * width, :],
                preferred_element_type=jnp.float32,
            )
    mean = jnp.sum(squares, axis=1, keepdims=True) / (count * width)
    own = x[me[0]].astype(jnp.float32)
    new[...] = (own + lax.rsqrt(mean + EPSILON) * total).astype(jnp.bfloat16)
    if receivers:
        for s in range(receivers):
            pltpu.make_async_copy(new, out.at[s], out_sems.at[s]).start()
        for s in range(receivers):
            pltpu.make_async_copy(new, out.at[s], out_sems.at[s]).wait()


def wide_layer(me, x, gain, w, receivers):
    count, rows, width = x.shape
    full, cols = w.shape
    chunks = 4
    dma = pltpu.SemaphoreType.DMA
    out_shape = [jax.ShapeDtypeStruct((rows, cols), x.dtype)]
    out_specs = [vmem()]
    scratch = [pltpu.VMEM(x.shape, x.dtype), pltpu.VMEM(w.shape, w.dtype), dma((chunks,)), dma((chunks,))]
    if receivers:
        out_shape.append(jax.ShapeDtypeStruct((receivers, rows, cols), x.dtype))
        out_specs.append(pl.BlockSpec(memory_space=pltpu.HBM))
        scratch.append(dma((receivers,)))

    def kernel(*refs):
        wide_kernel(*refs, receivers=receivers)

    return pl.pallas_call(
        kernel,
        out_shape=out_shape,
        in_specs=[smem(), hbm(), vmem(), hbm()],
        out_specs=out_specs,
        scratch_shapes=scratch,
        compiler_params=params(24),
        name="wide_layer",
    )(me, x, gain, w)


def fetch(parts, shape, use):
    def kernel(*refs):
        out, sems = refs[-2:]
        copies = [
            pltpu.make_async_copy(
                refs[i], out.at[parts[i][1], pl.ds(parts[i][2], parts[i][0].shape[0])], sems.at[n]
            )
            for n, i in enumerate(use)
        ]
        for copy in copies:
            copy.start()
        for copy in copies:
            copy.wait()

    return pl.pallas_call(
        kernel,
        out_shape=jax.ShapeDtypeStruct(shape, jnp.bfloat16),
        in_specs=[hbm()] * len(parts),
        out_specs=vmem(),
        scratch_shapes=[pltpu.SemaphoreType.DMA((len(use),))],
        compiler_params=params(24),
        cost_estimate=pl.CostEstimate(
            flops=0, bytes_accessed=shape[0] * shape[1] * shape[2] * 2, transcendentals=0
        ),
        name="fetch_weights",
    )(*[part for part, _, _ in parts])


def group_kernel(table, *refs, pieces, near):
    got, refs = refs[:pieces], refs[pieces:]
    gain, w, new, refs = refs[0], refs[1], refs[2], refs[3:]
    x = refs[-1]
    count, rows, width = x.shape
    if pieces == 1:
        x = got[0]
        for j in range(near):
            refs[0][j] = x[table[j]]
    else:
        for k in range(pieces):
            for j in range(near):
                x[table[k * near + j]] = got[k][j]
    squares = jnp.zeros((rows, width), jnp.float32)
    scaled = []
    for s in range(count):
        v = x[s].astype(jnp.float32)
        squares = squares + v * v
        scaled.append((v * gain[s : s + 1, :].astype(jnp.float32)).astype(jnp.bfloat16))
    scaled = jnp.concatenate(scaled, axis=1)
    inv = lax.rsqrt(jnp.sum(squares, axis=1, keepdims=True) / (count * width) + EPSILON)
    for j in range(near):
        total = jnp.dot(scaled, w[j], preferred_element_type=jnp.float32)
        new[j] = (x[table[j]].astype(jnp.float32) + inv * total).astype(jnp.bfloat16)


def group_layer(table, got, gain, w):
    near, full, cols = w.shape
    rows, width = got[0].shape[1:]
    count = full // width
    piece = jax.ShapeDtypeStruct((near, rows, cols), jnp.bfloat16)
    outs = 2 if len(got) == 1 else 1

    def kernel(*refs):
        group_kernel(*refs, pieces=len(got), near=near)

    return pl.pallas_call(
        kernel,
        out_shape=[piece] * outs,
        in_specs=[smem()] + [vmem()] * (len(got) + 2),
        out_specs=[vmem()] * outs,
        scratch_shapes=[pltpu.VMEM((count, rows, width), jnp.bfloat16)],
        compiler_params=params(24),
        name="group_layer",
    )(table, *got, gain, w)


def unset(*shapes):
    def kernel(*refs):
        pass

    return tuple(
        pl.pallas_call(
            kernel,
            out_shape=[jax.ShapeDtypeStruct(s, jnp.bfloat16) for s in shapes],
            out_specs=[hbm() for _ in shapes],
            name="unset",
        )()
    )


def error_kernel(x_hbm, gain, weights, keep, scaled, error_bf, loss, x, sems, *, sets):
    count, rows, width = x.shape
    copies = [pltpu.make_async_copy(x_hbm.at[s], x.at[s], sems.at[s]) for s in range(count)]
    for copy in copies:
        copy.start()
    for copy in copies:
        copy.wait()
    factors = []
    for first, size, where in sets:
        squares = jnp.zeros((size, width), jnp.float32)
        for s, (source, row) in enumerate(where):
            v = x[source, row : row + size, :].astype(jnp.float32)
            squares = squares + v * v
            scaled[s, first : first + size, :] = (v * gain[s : s + 1, :].astype(jnp.float32)).astype(
                jnp.bfloat16
            )
        mean = jnp.sum(squares, axis=1, keepdims=True) / (count * width)
        factors.append(lax.rsqrt(mean + EPSILON))
    inv = jnp.concatenate(factors, axis=0)
    total = jnp.zeros((rows, weights.shape[1]), jnp.float32)
    per = width // BLOCK
    for s in range(count):
        pruned = jnp.concatenate(
            [
                weights[i * BLOCK : (i + 1) * BLOCK, :]
                * (1 - keep[i : i + 1, :]).astype(jnp.bfloat16)
                for i in range(s * per, (s + 1) * per)
            ],
            axis=0,
        )
        total = total - jnp.dot(scaled[s], pruned, preferred_element_type=jnp.float32)
    error = inv * total
    rounded = error.astype(jnp.bfloat16).astype(jnp.float32)
    error_bf[...] = (rounded * inv).astype(jnp.bfloat16)
    part = jnp.sum(error * error, axis=0, keepdims=True)
    part = part[:, :128] + part[:, 128:]
    loss[...] = jnp.broadcast_to(part, loss.shape)


def layer_error(x, gain, weights, keep, sets):
    count, rows, width = x.shape
    cols = weights.shape[1]

    def kernel(*refs):
        error_kernel(*refs, sets=sets)

    return tuple(
        pl.pallas_call(
            kernel,
            out_shape=[
                jax.ShapeDtypeStruct((count, rows, width), jnp.bfloat16),
                jax.ShapeDtypeStruct((rows, cols), jnp.bfloat16),
                jax.ShapeDtypeStruct((8, 128), jnp.float32),
            ],
            in_specs=[hbm()] + [vmem()] * 3,
            out_specs=[vmem()] * 3,
            scratch_shapes=[pltpu.VMEM(x.shape, x.dtype), pltpu.SemaphoreType.DMA((count,))],
            compiler_params=params(24),
            name="layer_error",
        )(x, gain, weights, keep)
    )


def grad_kernel(normed, error_bf, keep, out, *, rows):
    width = normed.shape[2]
    per = width // BLOCK
    for s in range(normed.shape[0]):
        product = lax.dot_general(
            normed[s], error_bf[...], (((0,), (0,)), ((), ())), preferred_element_type=jnp.float32
        )
        for b in range(per):
            span = slice(b * BLOCK, (b + 1) * BLOCK)
            out[s * width + b * BLOCK : s * width + (b + 1) * BLOCK, :] = (
                product[span, :] * (1.0 / rows) * keep[s, b : b + 1, :]
            )


def layer_grad(normed, error_bf, keep, micro_rows):
    count, rows, width = normed.shape
    cols = error_bf.shape[1]
    step = 4

    def kernel(*refs):
        grad_kernel(*refs, rows=micro_rows)

    return pl.pallas_call(
        kernel,
        grid=(count // step,),
        out_shape=jax.ShapeDtypeStruct((count * width, cols), jnp.float32),
        in_specs=[
            pl.BlockSpec((step, rows, width), lambda s: (s, 0, 0)),
            pl.BlockSpec((rows, cols), lambda s: (0, 0)),
            pl.BlockSpec((step, width // BLOCK, cols), lambda s: (s, 0, 0)),
        ],
        out_specs=pl.BlockSpec((step * width, cols), lambda s: (s, 0)),
        compiler_params=params(24),
        name="layer_grad",
    )(normed, error_bf, keep.reshape(count, width // BLOCK, cols))


def shards(layer_input, weight, gain, block_mask):
    layers = lax.axis_size("layer")
    tensors = lax.axis_size("tensor")
    planes = layers // 2
    layer = lax.axis_index("layer")
    me = lax.axis_index("tensor").astype(jnp.int32)
    plane, core = layer // 2, layer % 2
    odd = core == 1
    my_x, my_y = me % SIDE, me // SIDE
    micro, micro_rows, width = layer_input.shape
    rows = micro * micro_rows
    weights = weight[0]
    full_width = weights.shape[0]
    group_rows = rows // SIDE
    piece = (SIDE, group_rows, width)
    half = full_width // 2

    def from_chip(value, shift):
        route = []
        for l in range(layers):
            for t in range(tensors):
                source = ((t // SIDE + shift[1]) % SIDE) * SIDE + (t % SIDE + shift[0]) % SIDE
                route.append((l * tensors + source, l * tensors + t))
        return lax.ppermute(value, AXES, route)

    def swap(value):
        route = [
            (l * tensors + t, (l ^ 1) * tensors + t) for l in range(layers) for t in range(tensors)
        ]
        return lax.ppermute(value, AXES, route)

    def hop(value, to, core=1):
        route = [
            ((2 * to - 1) * tensors + t, (2 * to + core) * tensors + t) for t in range(tensors)
        ]
        return lax.ppermute(value, AXES, route)

    def to_all(value):
        return lax.all_to_all(jnp.broadcast_to(value, (tensors,) + value.shape), "tensor", 0, 0)

    table = jnp.stack(
        [((my_y + j[1]) % SIDE) * SIDE + (my_x + k[0]) % SIDE for k in GROUP for j in NEAR]
    )
    here = me.reshape(1)
    own_gain = gain[0].reshape(tensors, width)
    other_gain = swap(own_gain)
    other_weights = swap(weights)

    held = (SIDE, full_width, width)
    part_shapes = [(half, width)] * 6
    gathered = (tensors, group_rows, width)

    def wide_plane(own):
        x = to_all(own)
        (middle,) = wide_layer(here, x, other_gain, other_weights, 0)
        (new,) = wide_layer(here, to_all(middle), own_gain, weights, 0)
        send = jnp.repeat(new.reshape(piece), SIDE, axis=0)
        return lax.all_to_all(send, "tensor", 0, 0), middle.reshape(piece)

    def first_plane():
        state = lax.cond(
            odd,
            lambda: wide_plane(layer_input.reshape(rows, width)),
            lambda: unset(gathered, piece),
        )
        return state + unset(*part_shapes, *part_shapes)

    def collect_weights():
        low, high = weights[:half], weights[half:]
        up_low, down_high = from_chip(low, (0, 1)), from_chip(high, (0, 3))
        up_high, down_low = from_chip(high, (0, 1)), from_chip(low, (0, 3))
        far_low, far_high = from_chip(up_low, (0, 1)), from_chip(down_high, (0, 3))
        mine = (up_low, up_high, down_low, down_high, far_low, far_high)
        return unset(gathered, piece) + mine + tuple(swap(part) for part in mine)

    new, middle, *parts = lax.cond(plane < 1, first_plane, collect_weights)
    before = layer_input.reshape(piece)
    spots = [(0, 0)] + [(slot, row) for slot in (1, 2, 3) for row in (0, half)]
    sources = [weights] + parts[:6] + [other_weights] + parts[6:]
    parts = [(source,) + spots[i % 7] for i, source in enumerate(sources)]
    mine, other = tuple(range(7)), tuple(range(7, 14))

    def exchange(own):
        return [own] + [from_chip(own, k) for k in GROUP[1:]]

    def group_plane(step, own):
        got = [own] if step == 1 else exchange(own)
        w = fetch(parts, held, other)
        middle, *first = group_layer(table, got, other_gain, w)
        own = first[0] if first else own
        if step == planes - 1:
            return middle
        w = fetch(parts, held, mine)
        (new,) = group_layer(table, exchange(middle), own_gain, w)
        return new, own, middle

    for step in range(1, planes - 1):
        came = hop(new, step)
        skipped = unset(piece)[0] if step == 1 else came
        new, before, middle = lax.cond(
            (plane == step) & odd,
            lambda came=came, step=step: group_plane(step, came),
            lambda new=skipped, a=before, b=middle: (new, a, b),
        )
    came = hop(new, planes - 1)
    for_even = hop(new, planes - 1, 0)

    own_piece = lax.cond(
        plane == planes - 1,
        lambda: lax.cond(odd, lambda: group_plane(planes - 1, came), lambda: for_even),
        lambda: jnp.where(odd, middle, swap(before)),
    )
    x = to_all(own_piece).reshape(tensors, rows, width)
    keep = jnp.repeat(block_mask[0].astype(jnp.float32), BLOCK, axis=1)
    wide_sets = [(0, rows, [(s, 0) for s in range(tensors)])]
    group_sets = []
    for y in range(SIDE):
        where = [None] * tensors
        for chip_x in range(SIDE):
            for j, (_, shift) in enumerate(NEAR):
                where[(y + shift) % SIDE * SIDE + chip_x] = (y * SIDE + chip_x, j * group_rows)
        group_sets.append((y * group_rows, group_rows, where))
    normed, error_bf, loss = lax.cond(
        plane < 1,
        lambda: layer_error(x, own_gain, weights, keep, wide_sets),
        lambda: layer_error(x, own_gain, weights, keep, group_sets),
    )
    shares = to_all(loss)
    grad = layer_grad(normed, error_bf, keep, micro_rows)
    total = jnp.sum(shares[:, 0, :]) / (micro_rows * full_width)
    return grad[None], total.reshape(1)


def solution(mesh):
    in_specs = (
        P(None, None, "tensor"),
        P("layer", None, "tensor"),
        P("layer", None),
        P("layer", None, "tensor"),
    )
    out_specs = (P("layer", None, "tensor"), P("layer"))
    return jax.shard_map(shards, mesh=mesh, in_specs=in_specs, out_specs=out_specs, check_vma=False)
```

```python
import jax
import jax.numpy as jnp
import numpy as np
from jax import lax
from jax.experimental import pallas as pl
from jax.experimental.pallas import tpu as pltpu
from jax.sharding import PartitionSpec as P

BLOCK = 128
EPSILON = 1e-05
AXES = ("layer", "tensor")
SIDE = 4
NEAR = ((0, 0), (0, 1), (0, 3), (0, 2))
GROUP = ((0, 0), (1, 0), (3, 0), (2, 0))
MIB = 1024 * 1024


def vmem():
    return pl.BlockSpec(memory_space=pltpu.VMEM)


def smem():
    return pl.BlockSpec(memory_space=pltpu.SMEM)


def hbm():
    return pl.BlockSpec(memory_space=pl.ANY)


def params(mib):
    return pltpu.CompilerParams(vmem_limit_bytes=mib * MIB)


def wide_kernel(me, x_hbm, gain, w_hbm, *refs, receivers):
    if receivers:
        new, out, x, w, x_sems, w_sems, out_sems = refs
    else:
        new, x, w, x_sems, w_sems = refs
    count, rows, width = x.shape
    chunks = x_sems.shape[0]
    per = count // chunks

    def x_copy(i):
        span = pl.ds(i * per, per)
        return pltpu.make_async_copy(x_hbm.at[span], x.at[span], x_sems.at[i])

    def w_copy(i):
        span = pl.ds(i * per * width, per * width)
        return pltpu.make_async_copy(w_hbm.at[span], w.at[span], w_sems.at[i])

    for i in range(chunks):
        x_copy(i).start()
        w_copy(i).start()
    squares = jnp.zeros((rows, width), jnp.float32)
    total = jnp.zeros((rows, w.shape[1]), jnp.float32)
    for i in range(chunks):
        x_copy(i).wait()
        w_copy(i).wait()
        for s in range(i * per, (i + 1) * per):
            v = x[s].astype(jnp.float32)
            squares = squares + v * v
            g = gain[s : s + 1, :].astype(jnp.float32)
            total = total + jnp.dot(
                (v * g).astype(jnp.bfloat16),
                w[s * width : (s + 1) * width, :],
                preferred_element_type=jnp.float32,
            )
    mean = jnp.sum(squares, axis=1, keepdims=True) / (count * width)
    own = x[me[0]].astype(jnp.float32)
    new[...] = (own + lax.rsqrt(mean + EPSILON) * total).astype(jnp.bfloat16)
    if receivers:
        for s in range(receivers):
            pltpu.make_async_copy(new, out.at[s], out_sems.at[s]).start()
        for s in range(receivers):
            pltpu.make_async_copy(new, out.at[s], out_sems.at[s]).wait()


def wide_layer(me, x, gain, w, receivers):
    count, rows, width = x.shape
    full, cols = w.shape
    chunks = 4
    dma = pltpu.SemaphoreType.DMA
    out_shape = [jax.ShapeDtypeStruct((rows, cols), x.dtype)]
    out_specs = [vmem()]
    scratch = [pltpu.VMEM(x.shape, x.dtype), pltpu.VMEM(w.shape, w.dtype), dma((chunks,)), dma((chunks,))]
    if receivers:
        out_shape.append(jax.ShapeDtypeStruct((receivers, rows, cols), x.dtype))
        out_specs.append(pl.BlockSpec(memory_space=pltpu.HBM))
        scratch.append(dma((receivers,)))

    def kernel(*refs):
        wide_kernel(*refs, receivers=receivers)

    return pl.pallas_call(
        kernel,
        out_shape=out_shape,
        in_specs=[smem(), hbm(), vmem(), hbm()],
        out_specs=out_specs,
        scratch_shapes=scratch,
        compiler_params=params(24),
        name="wide_layer",
    )(me, x, gain, w)


def fetch(parts, shape, use):
    def kernel(*refs):
        out, sems = refs[-2:]
        copies = [
            pltpu.make_async_copy(
                refs[i], out.at[parts[i][1], pl.ds(parts[i][2], parts[i][0].shape[0])], sems.at[n]
            )
            for n, i in enumerate(use)
        ]
        for copy in copies:
            copy.start()
        for copy in copies:
            copy.wait()

    return pl.pallas_call(
        kernel,
        out_shape=jax.ShapeDtypeStruct(shape, jnp.bfloat16),
        in_specs=[hbm()] * len(parts),
        out_specs=vmem(),
        scratch_shapes=[pltpu.SemaphoreType.DMA((len(use),))],
        compiler_params=params(24),
        cost_estimate=pl.CostEstimate(
            flops=0, bytes_accessed=shape[0] * shape[1] * shape[2] * 2, transcendentals=0
        ),
        name="fetch_weights",
    )(*[part for part, _, _ in parts])


def group_kernel(table, *refs, pieces, near):
    got, refs = refs[:pieces], refs[pieces:]
    gain, w, new, refs = refs[0], refs[1], refs[2], refs[3:]
    x = refs[-1]
    count, rows, width = x.shape
    if pieces == 1:
        x = got[0]
        for j in range(near):
            refs[0][j] = x[table[j]]
    else:
        for k in range(pieces):
            for j in range(near):
                x[table[k * near + j]] = got[k][j]
    squares = jnp.zeros((rows, width), jnp.float32)
    scaled = []
    for s in range(count):
        v = x[s].astype(jnp.float32)
        squares = squares + v * v
        scaled.append((v * gain[s : s + 1, :].astype(jnp.float32)).astype(jnp.bfloat16))
    scaled = jnp.concatenate(scaled, axis=1)
    inv = lax.rsqrt(jnp.sum(squares, axis=1, keepdims=True) / (count * width) + EPSILON)
    for j in range(near):
        total = jnp.dot(scaled, w[j], preferred_element_type=jnp.float32)
        new[j] = (x[table[j]].astype(jnp.float32) + inv * total).astype(jnp.bfloat16)


def group_layer(table, got, gain, w):
    near, full, cols = w.shape
    rows, width = got[0].shape[1:]
    count = full // width
    piece = jax.ShapeDtypeStruct((near, rows, cols), jnp.bfloat16)
    outs = 2 if len(got) == 1 else 1

    def kernel(*refs):
        group_kernel(*refs, pieces=len(got), near=near)

    return pl.pallas_call(
        kernel,
        out_shape=[piece] * outs,
        in_specs=[smem()] + [vmem()] * (len(got) + 2),
        out_specs=[vmem()] * outs,
        scratch_shapes=[pltpu.VMEM((count, rows, width), jnp.bfloat16)],
        compiler_params=params(24),
        name="group_layer",
    )(table, *got, gain, w)


def unset(*shapes):
    def kernel(*refs):
        pass

    return tuple(
        pl.pallas_call(
            kernel,
            out_shape=[jax.ShapeDtypeStruct(s, jnp.bfloat16) for s in shapes],
            out_specs=[hbm() for _ in shapes],
            name="unset",
        )()
    )


def prune_kernel(weights, keep, out):
    for i in range(keep.shape[0]):
        span = slice(i * BLOCK, (i + 1) * BLOCK)
        out[span, :] = weights[span, :] * (1 - keep[i : i + 1, :]).astype(jnp.bfloat16)


def prune(weights, keep):
    return pl.pallas_call(
        prune_kernel,
        out_shape=jax.ShapeDtypeStruct(weights.shape, weights.dtype),
        in_specs=[vmem()] * 2,
        out_specs=vmem(),
        compiler_params=params(12),
        cost_estimate=pl.CostEstimate(
            flops=weights.size, bytes_accessed=weights.size * 4, transcendentals=0
        ),
        name="prune",
    )(weights, keep)


def set_rows(where, x, size, y, s):
    return x[where[0, y, s], pl.ds(pl.multiple_of(where[1, y, s], size), size), :].astype(jnp.float32)


def error_kernel(where, x, gain, pruned_hbm, error_bf, loss, scaled, pruned, sem):
    fetch_pruned = pltpu.make_async_copy(pruned_hbm, pruned, sem)
    fetch_pruned.start()
    count, rows, width = x.shape
    sets = where.shape[1]
    size = rows // sets
    factors = []
    for y in range(sets):
        squares = jnp.zeros((size, width), jnp.float32)
        for s in range(count):
            v = set_rows(where, x, size, y, s)
            squares = squares + v * v
            scaled[y * size : (y + 1) * size, s * width : (s + 1) * width] = (
                v * gain[s : s + 1, :].astype(jnp.float32)
            ).astype(jnp.bfloat16)
        mean = jnp.sum(squares, axis=1, keepdims=True) / (count * width)
        factors.append(lax.rsqrt(mean + EPSILON))
    inv = jnp.concatenate(factors, axis=0)
    fetch_pruned.wait()
    error = -inv * jnp.dot(scaled[...], pruned[...], preferred_element_type=jnp.float32)
    rounded = error.astype(jnp.bfloat16).astype(jnp.float32)
    error_bf[...] = (rounded * inv).astype(jnp.bfloat16)
    part = jnp.sum(error * error, axis=0, keepdims=True)
    part = part[:, :128] + part[:, 128:]
    loss[...] = jnp.broadcast_to(part, loss.shape)


def layer_error(where, x, gain, pruned):
    count, rows, width = x.shape
    cols = pruned.shape[1]
    return pl.pallas_call(
        error_kernel,
        out_shape=[
            jax.ShapeDtypeStruct((rows, cols), jnp.bfloat16),
            jax.ShapeDtypeStruct((16, 8, 128), jnp.float32),
        ],
        in_specs=[smem()] + [vmem()] * 2 + [hbm()],
        out_specs=[vmem()] * 2,
        scratch_shapes=[
            pltpu.VMEM((rows, count * width), jnp.bfloat16),
            pltpu.VMEM(pruned.shape, pruned.dtype),
            pltpu.SemaphoreType.DMA,
        ],
        compiler_params=params(16),
        name="layer_error",
    )(where, x, gain, pruned)


def grad_kernel(where, x, gain, error_bf, keep, out, *, step, micro_rows):
    count, rows, width = x.shape
    sets = where.shape[1]
    size = rows // sets
    per = width // BLOCK
    first = pl.program_id(0) * step
    for n in range(step):
        s = first + n
        g = gain[pl.ds(s, 1), :].astype(jnp.float32)
        scaled = jnp.concatenate(
            [(set_rows(where, x, size, y, s) * g).astype(jnp.bfloat16) for y in range(sets)], axis=0
        )
        product = lax.dot_general(
            scaled, error_bf[...], (((0,), (0,)), ((), ())), preferred_element_type=jnp.float32
        )
        for b in range(per):
            out[n * width + b * BLOCK : n * width + (b + 1) * BLOCK, :] = (
                product[b * BLOCK : (b + 1) * BLOCK, :]
                * (1.0 / micro_rows)
                * keep[pl.ds(s * per + b, 1), :]
            )


def layer_grad(where, x, gain, error_bf, keep, micro_rows):
    count, rows, width = x.shape
    cols = error_bf.shape[1]
    step = 4

    def kernel(*refs):
        grad_kernel(*refs, step=step, micro_rows=micro_rows)

    return pl.pallas_call(
        kernel,
        grid=(count // step,),
        out_shape=jax.ShapeDtypeStruct((count * width, cols), jnp.float32),
        in_specs=[smem()] + [vmem()] * 4,
        out_specs=pl.BlockSpec((step * width, cols), lambda s: (s, 0)),
        compiler_params=params(16),
        name="layer_grad",
    )(where, x, gain, error_bf, keep)


def shards(layer_input, weight, gain, block_mask):
    layers = lax.axis_size("layer")
    tensors = lax.axis_size("tensor")
    planes = layers // 2
    layer = lax.axis_index("layer")
    me = lax.axis_index("tensor").astype(jnp.int32)
    plane, core = layer // 2, layer % 2
    odd = core == 1
    my_x, my_y = me % SIDE, me // SIDE
    micro, micro_rows, width = layer_input.shape
    rows = micro * micro_rows
    weights = weight[0]
    full_width = weights.shape[0]
    group_rows = rows // SIDE
    piece = (SIDE, group_rows, width)
    half = full_width // 2

    def from_chip(value, shift):
        route = []
        for l in range(layers):
            for t in range(tensors):
                source = ((t // SIDE + shift[1]) % SIDE) * SIDE + (t % SIDE + shift[0]) % SIDE
                route.append((l * tensors + source, l * tensors + t))
        return lax.ppermute(value, AXES, route)

    def swap(value):
        route = [
            (l * tensors + t, (l ^ 1) * tensors + t) for l in range(layers) for t in range(tensors)
        ]
        return lax.ppermute(value, AXES, route)

    def hop(value, to, core=1):
        route = [
            ((2 * to - 1) * tensors + t, (2 * to + core) * tensors + t) for t in range(tensors)
        ]
        return lax.ppermute(value, AXES, route)

    def to_all(value):
        return lax.all_to_all(jnp.broadcast_to(value, (tensors,) + value.shape), "tensor", 0, 0)

    table = jnp.stack(
        [((my_y + j[1]) % SIDE) * SIDE + (my_x + k[0]) % SIDE for k in GROUP for j in NEAR]
    )
    here = me.reshape(1)
    own_gain = gain[0].reshape(tensors, width)

    other_gain = swap(own_gain)
    other_weights = swap(weights)
    held = (SIDE, full_width, width)
    part_shapes = [(half, width)] * 6
    gathered = (tensors, group_rows, width)

    def wide_plane(own):
        x = to_all(own)
        (middle,) = wide_layer(here, x, other_gain, other_weights, 0)
        (new,) = wide_layer(here, to_all(middle), own_gain, weights, 0)
        send = jnp.repeat(new.reshape(piece), SIDE, axis=0)
        return lax.all_to_all(send, "tensor", 0, 0), middle.reshape(piece)

    def first_plane():
        state = lax.cond(
            odd,
            lambda: wide_plane(layer_input.reshape(rows, width)),
            lambda: unset(gathered, piece),
        )
        return state + unset(*part_shapes, *part_shapes)

    def collect_weights():
        low, high = weights[:half], weights[half:]
        up_low, down_high = from_chip(low, (0, 1)), from_chip(high, (0, 3))
        up_high, down_low = from_chip(high, (0, 1)), from_chip(low, (0, 3))
        far_low, far_high = from_chip(up_low, (0, 1)), from_chip(down_high, (0, 3))
        mine = (up_low, up_high, down_low, down_high, far_low, far_high)
        return unset(gathered, piece) + mine + tuple(swap(part) for part in mine)

    new, middle, *parts = lax.cond(plane < 1, first_plane, collect_weights)
    before = middle
    spots = [(0, 0)] + [(slot, row) for slot in (1, 2, 3) for row in (0, half)]
    sources = [weights] + parts[:6] + [other_weights] + parts[6:]
    parts = [(source,) + spots[i % 7] for i, source in enumerate(sources)]
    mine, other = tuple(range(7)), tuple(range(7, 14))

    def exchange(own):
        return [own] + [from_chip(own, k) for k in GROUP[1:]]

    def group_plane(step, own):
        got = [own] if step == 1 else exchange(own)
        w = fetch(parts, held, other)
        middle, *first = group_layer(table, got, other_gain, w)
        own = first[0] if first else own
        if step == planes - 1:
            return middle
        w = fetch(parts, held, mine)
        (new,) = group_layer(table, exchange(middle), own_gain, w)
        return new, own, middle

    for step in range(1, planes - 1):
        came = hop(new, step)
        skipped = unset(piece)[0] if step == 1 else came
        new, before, middle = lax.cond(
            (plane == step) & odd,
            lambda came=came, step=step: group_plane(step, came),
            lambda new=skipped, a=before, b=middle: (new, a, b),
        )
    came = hop(new, planes - 1)
    for_even = hop(new, planes - 1, 0)

    own_piece = lax.cond(
        plane == planes - 1,
        lambda: lax.cond(odd, lambda: group_plane(planes - 1, came), lambda: for_even),
        lambda: jnp.where(
            odd, middle, jnp.where(plane == 0, layer_input.reshape(piece), swap(before))
        ),
    )
    keep = jnp.repeat(block_mask[0].astype(jnp.float32), BLOCK, axis=1)
    wide_table = np.zeros((2, SIDE, tensors), np.int32)
    group_table = np.zeros((2, SIDE, tensors), np.int32)
    for y in range(SIDE):
        for s in range(tensors):
            wide_table[:, y, s] = s, y * group_rows
            for j, (_, shift) in enumerate(NEAR):
                if (y + shift) % SIDE == s // SIDE:
                    group_table[:, y, s] = y * SIDE + s % SIDE, j * group_rows
    where = jnp.where(plane < 1, jnp.asarray(wide_table), jnp.asarray(group_table))
    full_gain = own_gain.astype(jnp.float32)
    send = jnp.broadcast_to(own_piece, (tensors,) + own_piece.shape)
    send, late_weights = lax.optimization_barrier((send, weights))
    x = lax.all_to_all(send, "tensor", 0, 0).reshape(tensors, rows, width)
    pruned = prune(late_weights, keep)
    error_bf, loss = layer_error(where, x, full_gain, pruned)
    shares = lax.all_to_all(loss, "tensor", 0, 0)
    grad = layer_grad(where, x, full_gain, error_bf, keep, micro_rows)
    total = jnp.sum(shares[:, 0, :]) / (micro_rows * full_width)
    return grad[None], total.reshape(1)


def solution(mesh):
    in_specs = (
        P(None, None, "tensor"),
        P("layer", None, "tensor"),
        P("layer", None),
        P("layer", None, "tensor"),
    )
    out_specs = (P("layer", None, "tensor"), P("layer"))
    return jax.shard_map(shards, mesh=mesh, in_specs=in_specs, out_specs=out_specs, check_vma=False)
```

```python
import jax
import jax.numpy as jnp
import numpy as np
from jax import lax
from jax.experimental import pallas as pl
from jax.experimental.pallas import tpu as pltpu
from jax.sharding import PartitionSpec as P

BLOCK = 128
EPSILON = 1e-05
AXES = ("layer", "tensor")
SIDE = 4
NEAR = ((0, 0), (0, 1), (0, 3), (0, 2))
GROUP = ((0, 0), (1, 0), (3, 0), (2, 0))
MIB = 1024 * 1024


def vmem():
    return pl.BlockSpec(memory_space=pltpu.VMEM)


def smem():
    return pl.BlockSpec(memory_space=pltpu.SMEM)


def hbm():
    return pl.BlockSpec(memory_space=pl.ANY)


def params(mib):
    return pltpu.CompilerParams(vmem_limit_bytes=mib * MIB)


def wide_kernel(me, x_hbm, gain, w_hbm, *refs, receivers):
    if receivers:
        new, out, x, w, x_sems, w_sems, out_sems = refs
    else:
        new, x, w, x_sems, w_sems = refs
    count, rows, width = x.shape
    chunks = x_sems.shape[0]
    per = count // chunks

    def x_copy(i):
        span = pl.ds(i * per, per)
        return pltpu.make_async_copy(x_hbm.at[span], x.at[span], x_sems.at[i])

    def w_copy(i):
        span = pl.ds(i * per * width, per * width)
        return pltpu.make_async_copy(w_hbm.at[span], w.at[span], w_sems.at[i])

    for i in range(chunks):
        x_copy(i).start()
        w_copy(i).start()
    squares = jnp.zeros((rows, width), jnp.float32)
    total = jnp.zeros((rows, w.shape[1]), jnp.float32)
    for i in range(chunks):
        x_copy(i).wait()
        w_copy(i).wait()
        for s in range(i * per, (i + 1) * per):
            v = x[s].astype(jnp.float32)
            squares = squares + v * v
            g = gain[s : s + 1, :].astype(jnp.float32)
            total = total + jnp.dot(
                (v * g).astype(jnp.bfloat16),
                w[s * width : (s + 1) * width, :],
                preferred_element_type=jnp.float32,
            )
    mean = jnp.sum(squares, axis=1, keepdims=True) / (count * width)
    own = x[me[0]].astype(jnp.float32)
    new[...] = (own + lax.rsqrt(mean + EPSILON) * total).astype(jnp.bfloat16)
    if receivers:
        for s in range(receivers):
            pltpu.make_async_copy(new, out.at[s], out_sems.at[s]).start()
        for s in range(receivers):
            pltpu.make_async_copy(new, out.at[s], out_sems.at[s]).wait()


def wide_layer(me, x, gain, w, receivers):
    count, rows, width = x.shape
    full, cols = w.shape
    chunks = 4
    dma = pltpu.SemaphoreType.DMA
    out_shape = [jax.ShapeDtypeStruct((rows, cols), x.dtype)]
    out_specs = [vmem()]
    scratch = [pltpu.VMEM(x.shape, x.dtype), pltpu.VMEM(w.shape, w.dtype), dma((chunks,)), dma((chunks,))]
    if receivers:
        out_shape.append(jax.ShapeDtypeStruct((receivers, rows, cols), x.dtype))
        out_specs.append(pl.BlockSpec(memory_space=pltpu.HBM))
        scratch.append(dma((receivers,)))

    def kernel(*refs):
        wide_kernel(*refs, receivers=receivers)

    return pl.pallas_call(
        kernel,
        out_shape=out_shape,
        in_specs=[smem(), hbm(), vmem(), hbm()],
        out_specs=out_specs,
        scratch_shapes=scratch,
        compiler_params=params(24),
        name="wide_layer",
    )(me, x, gain, w)


def fetch(parts, shape, use):
    def kernel(*refs):
        out, sems = refs[-2:]
        copies = [
            pltpu.make_async_copy(
                refs[i], out.at[parts[i][1], pl.ds(parts[i][2], parts[i][0].shape[0])], sems.at[n]
            )
            for n, i in enumerate(use)
        ]
        for copy in copies:
            copy.start()
        for copy in copies:
            copy.wait()

    return pl.pallas_call(
        kernel,
        out_shape=jax.ShapeDtypeStruct(shape, jnp.bfloat16),
        in_specs=[hbm()] * len(parts),
        out_specs=vmem(),
        scratch_shapes=[pltpu.SemaphoreType.DMA((len(use),))],
        compiler_params=params(24),
        cost_estimate=pl.CostEstimate(
            flops=0, bytes_accessed=shape[0] * shape[1] * shape[2] * 2, transcendentals=0
        ),
        name="fetch_weights",
    )(*[part for part, _, _ in parts])


def group_kernel(table, *refs, pieces, near, spots):
    got, refs = refs[:pieces], refs[pieces:]
    gain, refs = refs[0], refs[1:]
    copies = []
    if spots:
        sources, refs = refs[: len(spots)], refs[len(spots) :]
        w, sems, refs = refs[-2], refs[-1], refs[:-2]
        copies = [
            pltpu.make_async_copy(
                source, w.at[slot, pl.ds(row, source.shape[0])], sems.at[n]
            )
            for n, (source, (slot, row)) in enumerate(zip(sources, spots))
        ]
        for copy in copies:
            copy.start()
    else:
        w, refs = refs[0], refs[1:]
    new, refs = refs[0], refs[1:]
    x = refs[-1]
    count, rows, width = x.shape
    if pieces == 1:
        x = got[0]
        for j in range(near):
            refs[0][j] = x[table[j]]
    else:
        for k in range(pieces):
            for j in range(near):
                x[table[k * near + j]] = got[k][j]
    squares = jnp.zeros((rows, width), jnp.float32)
    scaled = []
    for s in range(count):
        v = x[s].astype(jnp.float32)
        squares = squares + v * v
        scaled.append((v * gain[s : s + 1, :].astype(jnp.float32)).astype(jnp.bfloat16))
    scaled = jnp.concatenate(scaled, axis=1)
    inv = lax.rsqrt(jnp.sum(squares, axis=1, keepdims=True) / (count * width) + EPSILON)
    for j in range(near):
        for copy, (slot, _) in zip(copies, spots):
            if slot == j:
                copy.wait()
        total = jnp.dot(scaled, w[j], preferred_element_type=jnp.float32)
        new[j] = (x[table[j]].astype(jnp.float32) + inv * total).astype(jnp.bfloat16)


def group_layer(table, got, gain, w=None, parts=(), shape=None):
    near, full, cols = w.shape if shape is None else shape
    rows, width = got[0].shape[1:]
    count = full // width
    piece = jax.ShapeDtypeStruct((near, rows, cols), jnp.bfloat16)
    outs = 2 if len(got) == 1 else 1

    def kernel(*refs):
        group_kernel(
            *refs, pieces=len(got), near=near, spots=[(slot, row) for _, slot, row in parts]
        )

    scratch = [pltpu.VMEM((count, rows, width), jnp.bfloat16)]
    if parts:
        scratch += [pltpu.VMEM(shape, jnp.bfloat16), pltpu.SemaphoreType.DMA((len(parts),))]
        held, specs = [part for part, _, _ in parts], [hbm()] * len(parts)
    else:
        held, specs = [w], [vmem()]
    return pl.pallas_call(
        kernel,
        out_shape=[piece] * outs,
        in_specs=[smem()] + [vmem()] * (len(got) + 1) + specs,
        out_specs=[vmem()] * outs,
        scratch_shapes=scratch,
        compiler_params=params(24),
        name="group_layer",
    )(table, *got, gain, *held)


def unset(*shapes):
    def kernel(*refs):
        pass

    return tuple(
        pl.pallas_call(
            kernel,
            out_shape=[jax.ShapeDtypeStruct(s, jnp.bfloat16) for s in shapes],
            out_specs=[hbm() for _ in shapes],
            name="unset",
        )()
    )


def prune_kernel(weights, keep, out):
    for i in range(keep.shape[0]):
        span = slice(i * BLOCK, (i + 1) * BLOCK)
        out[span, :] = weights[span, :] * (1 - keep[i : i + 1, :]).astype(jnp.bfloat16)


def prune(weights, keep):
    return pl.pallas_call(
        prune_kernel,
        out_shape=jax.ShapeDtypeStruct(weights.shape, weights.dtype),
        in_specs=[vmem()] * 2,
        out_specs=vmem(),
        compiler_params=params(12),
        cost_estimate=pl.CostEstimate(
            flops=weights.size, bytes_accessed=weights.size * 4, transcendentals=0
        ),
        name="prune",
    )(weights, keep)


def set_rows(where, x, size, y, s):
    return x[where[0, y, s], pl.ds(pl.multiple_of(where[1, y, s], size), size), :].astype(jnp.float32)


def error_kernel(where, x, gain, pruned_hbm, error_bf, loss, scaled, pruned, sem):
    fetch_pruned = pltpu.make_async_copy(pruned_hbm, pruned, sem)
    fetch_pruned.start()
    count, rows, width = x.shape
    sets = where.shape[1]
    size = rows // sets
    factors = []
    for y in range(sets):
        squares = jnp.zeros((size, width), jnp.float32)
        for s in range(count):
            v = set_rows(where, x, size, y, s)
            squares = squares + v * v
            scaled[y * size : (y + 1) * size, s * width : (s + 1) * width] = (
                v * gain[s : s + 1, :].astype(jnp.float32)
            ).astype(jnp.bfloat16)
        mean = jnp.sum(squares, axis=1, keepdims=True) / (count * width)
        factors.append(lax.rsqrt(mean + EPSILON))
    inv = jnp.concatenate(factors, axis=0)
    fetch_pruned.wait()
    error = -inv * jnp.dot(scaled[...], pruned[...], preferred_element_type=jnp.float32)
    rounded = error.astype(jnp.bfloat16).astype(jnp.float32)
    error_bf[...] = (rounded * inv).astype(jnp.bfloat16)
    part = jnp.sum(error * error, axis=0, keepdims=True)
    part = part[:, :128] + part[:, 128:]
    loss[...] = jnp.broadcast_to(part, loss.shape)


def layer_error(where, x, gain, pruned):
    count, rows, width = x.shape
    cols = pruned.shape[1]
    return pl.pallas_call(
        error_kernel,
        out_shape=[
            jax.ShapeDtypeStruct((rows, cols), jnp.bfloat16),
            jax.ShapeDtypeStruct((16, 8, 128), jnp.float32),
        ],
        in_specs=[smem()] + [vmem()] * 2 + [hbm()],
        out_specs=[vmem()] * 2,
        scratch_shapes=[
            pltpu.VMEM((rows, count * width), jnp.bfloat16),
            pltpu.VMEM(pruned.shape, pruned.dtype),
            pltpu.SemaphoreType.DMA,
        ],
        compiler_params=params(16),
        name="layer_error",
    )(where, x, gain, pruned)


def grad_kernel(where, x, gain, error_bf, keep, out, *, step, micro_rows):
    count, rows, width = x.shape
    sets = where.shape[1]
    size = rows // sets
    per = width // BLOCK
    first = pl.program_id(0) * step
    for n in range(step):
        s = first + n
        g = gain[pl.ds(s, 1), :].astype(jnp.float32)
        scaled = jnp.concatenate(
            [(set_rows(where, x, size, y, s) * g).astype(jnp.bfloat16) for y in range(sets)], axis=0
        )
        product = lax.dot_general(
            scaled, error_bf[...], (((0,), (0,)), ((), ())), preferred_element_type=jnp.float32
        )
        for b in range(per):
            out[n * width + b * BLOCK : n * width + (b + 1) * BLOCK, :] = (
                product[b * BLOCK : (b + 1) * BLOCK, :]
                * (1.0 / micro_rows)
                * keep[pl.ds(s * per + b, 1), :]
            )


def layer_grad(where, x, gain, error_bf, keep, micro_rows):
    count, rows, width = x.shape
    cols = error_bf.shape[1]
    step = 4

    def kernel(*refs):
        grad_kernel(*refs, step=step, micro_rows=micro_rows)

    return pl.pallas_call(
        kernel,
        grid=(count // step,),
        out_shape=jax.ShapeDtypeStruct((count * width, cols), jnp.float32),
        in_specs=[smem()] + [vmem()] * 4,
        out_specs=pl.BlockSpec((step * width, cols), lambda s: (s, 0)),
        compiler_params=params(16),
        name="layer_grad",
    )(where, x, gain, error_bf, keep)


def shards(layer_input, weight, gain, block_mask):
    layers = lax.axis_size("layer")
    tensors = lax.axis_size("tensor")
    planes = layers // 2
    layer = lax.axis_index("layer")
    me = lax.axis_index("tensor").astype(jnp.int32)
    plane, core = layer // 2, layer % 2
    odd = core == 1
    my_x, my_y = me % SIDE, me // SIDE
    micro, micro_rows, width = layer_input.shape
    rows = micro * micro_rows
    weights = weight[0]
    full_width = weights.shape[0]
    group_rows = rows // SIDE
    piece = (SIDE, group_rows, width)
    half = full_width // 2

    def from_chip(value, shift):
        route = []
        for l in range(layers):
            for t in range(tensors):
                source = ((t // SIDE + shift[1]) % SIDE) * SIDE + (t % SIDE + shift[0]) % SIDE
                route.append((l * tensors + source, l * tensors + t))
        return lax.ppermute(value, AXES, route)

    def swap(value):
        route = [
            (l * tensors + t, (l ^ 1) * tensors + t) for l in range(layers) for t in range(tensors)
        ]
        return lax.ppermute(value, AXES, route)

    def hop(value, to, core=1):
        route = [
            ((2 * to - 1) * tensors + t, (2 * to + core) * tensors + t) for t in range(tensors)
        ]
        return lax.ppermute(value, AXES, route)

    def to_all(value):
        return lax.all_to_all(jnp.broadcast_to(value, (tensors,) + value.shape), "tensor", 0, 0)

    table = jnp.stack(
        [((my_y + j[1]) % SIDE) * SIDE + (my_x + k[0]) % SIDE for k in GROUP for j in NEAR]
    )
    here = me.reshape(1)
    own_gain = gain[0].reshape(tensors, width)

    other_gain = swap(own_gain)
    other_weights = swap(weights)
    held = (SIDE, full_width, width)
    part_shapes = [(half, width)] * 6
    gathered = (tensors, group_rows, width)

    def wide_plane(own):
        x = to_all(own)
        (middle,) = wide_layer(here, x, other_gain, other_weights, 0)
        (new,) = wide_layer(here, to_all(middle), own_gain, weights, 0)
        send = jnp.repeat(new.reshape(piece), SIDE, axis=0)
        return lax.all_to_all(send, "tensor", 0, 0), middle.reshape(piece)

    def first_plane():
        state = lax.cond(
            odd,
            lambda: wide_plane(layer_input.reshape(rows, width)),
            lambda: unset(gathered, piece),
        )
        return state + unset(*part_shapes, *part_shapes)

    def collect_weights():
        low, high = weights[:half], weights[half:]
        up_low, down_high = from_chip(low, (0, 1)), from_chip(high, (0, 3))
        up_high, down_low = from_chip(high, (0, 1)), from_chip(low, (0, 3))
        far_low, far_high = from_chip(up_low, (0, 1)), from_chip(down_high, (0, 3))
        mine = (up_low, up_high, down_low, down_high, far_low, far_high)
        return unset(gathered, piece) + mine + tuple(swap(part) for part in mine)

    new, middle, *parts = lax.cond(plane < 1, first_plane, collect_weights)
    before = middle
    spots = [(0, 0)] + [(slot, row) for slot in (1, 2, 3) for row in (0, half)]
    sources = [weights] + parts[:6] + [other_weights] + parts[6:]
    parts = [(source,) + spots[i % 7] for i, source in enumerate(sources)]
    mine, other = tuple(range(7)), tuple(range(7, 14))

    def exchange(own):
        return [own] + [from_chip(own, k) for k in GROUP[1:]]

    def group_plane(step, own):
        if step == 1:
            middle, own = group_layer(
                table, [own], other_gain, parts=[parts[i] for i in other], shape=held
            )
        else:
            got = exchange(own)
            w = fetch(parts, held, other)
            (middle,) = group_layer(table, got, other_gain, w)
        if step == planes - 1:
            return middle
        w = fetch(parts, held, mine)
        (new,) = group_layer(table, exchange(middle), own_gain, w)
        return new, own, middle

    for step in range(1, planes - 1):
        came = hop(new, step)
        skipped = unset(piece)[0] if step == 1 else came
        if step == planes - 2:
            before_last = hop(new, step, 0)
        new, before, middle = lax.cond(
            (plane == step) & odd,
            lambda came=came, step=step: group_plane(step, came),
            lambda new=skipped, a=before, b=middle: (new, a, b),
        )
    came = hop(new, planes - 1)
    for_even = hop(new, planes - 1, 0)

    def piece_of_plane():
        even = lax.cond(plane == planes - 2, lambda: before_last, lambda: swap(before))
        return jnp.where(odd, middle, jnp.where(plane == 0, layer_input.reshape(piece), even))

    own_piece = lax.cond(
        plane == planes - 1,
        lambda: lax.cond(odd, lambda: group_plane(planes - 1, came), lambda: for_even),
        piece_of_plane,
    )
    keep = jnp.repeat(block_mask[0].astype(jnp.float32), BLOCK, axis=1)
    wide_table = np.zeros((2, SIDE, tensors), np.int32)
    group_table = np.zeros((2, SIDE, tensors), np.int32)
    for y in range(SIDE):
        for s in range(tensors):
            wide_table[:, y, s] = s, y * group_rows
            for j, (_, shift) in enumerate(NEAR):
                if (y + shift) % SIDE == s // SIDE:
                    group_table[:, y, s] = y * SIDE + s % SIDE, j * group_rows
    where = jnp.where(plane < 1, jnp.asarray(wide_table), jnp.asarray(group_table))
    full_gain = own_gain.astype(jnp.float32)
    send = jnp.broadcast_to(own_piece, (tensors,) + own_piece.shape)
    send, late_weights = lax.optimization_barrier((send, weights))
    x = lax.all_to_all(send, "tensor", 0, 0).reshape(tensors, rows, width)
    pruned = prune(late_weights, keep)
    error_bf, loss = layer_error(where, x, full_gain, pruned)
    shares = lax.all_to_all(loss, "tensor", 0, 0)
    grad = layer_grad(where, x, full_gain, error_bf, keep, micro_rows)
    total = jnp.sum(shares[:, 0, :]) / (micro_rows * full_width)
    return grad[None], total.reshape(1)


def solution(mesh):
    in_specs = (
        P(None, None, "tensor"),
        P("layer", None, "tensor"),
        P("layer", None),
        P("layer", None, "tensor"),
    )
    out_specs = (P("layer", None, "tensor"), P("layer"))
    return jax.shard_map(shards, mesh=mesh, in_specs=in_specs, out_specs=out_specs, check_vma=False)
```

```python
import jax
import jax.numpy as jnp
import numpy as np
from jax import lax
from jax.experimental import pallas as pl
from jax.experimental.pallas import tpu as pltpu
from jax.sharding import PartitionSpec as P

BLOCK = 128
EPSILON = 1e-05
AXES = ("layer", "tensor")
SIDE = 4
NEAR = ((0, 0), (0, 1), (0, 3), (0, 2))
GROUP = ((0, 0), (1, 0), (3, 0), (2, 0))
MIB = 1024 * 1024


def vmem():
    return pl.BlockSpec(memory_space=pltpu.VMEM)


def smem():
    return pl.BlockSpec(memory_space=pltpu.SMEM)


def hbm():
    return pl.BlockSpec(memory_space=pl.ANY)


def params(mib):
    return pltpu.CompilerParams(vmem_limit_bytes=mib * MIB)


def wide_kernel(me, x_hbm, gain, w_hbm, *refs, receivers):
    if receivers:
        new, out, x, w, x_sems, w_sems, out_sems = refs
    else:
        new, x, w, x_sems, w_sems = refs
    count, rows, width = x.shape
    chunks = x_sems.shape[0]
    per = count // chunks

    def x_copy(i):
        span = pl.ds(i * per, per)
        return pltpu.make_async_copy(x_hbm.at[span], x.at[span], x_sems.at[i])

    def w_copy(i):
        span = pl.ds(i * per * width, per * width)
        return pltpu.make_async_copy(w_hbm.at[span], w.at[span], w_sems.at[i])

    for i in range(chunks):
        x_copy(i).start()
        w_copy(i).start()
    squares = jnp.zeros((rows, width), jnp.float32)
    total = jnp.zeros((rows, w.shape[1]), jnp.float32)
    for i in range(chunks):
        x_copy(i).wait()
        w_copy(i).wait()
        for s in range(i * per, (i + 1) * per):
            v = x[s].astype(jnp.float32)
            squares = squares + v * v
            g = gain[s : s + 1, :].astype(jnp.float32)
            total = total + jnp.dot(
                (v * g).astype(jnp.bfloat16),
                w[s * width : (s + 1) * width, :],
                preferred_element_type=jnp.float32,
            )
    mean = jnp.sum(squares, axis=1, keepdims=True) / (count * width)
    own = x[me[0]].astype(jnp.float32)
    new[...] = (own + lax.rsqrt(mean + EPSILON) * total).astype(jnp.bfloat16)
    if receivers:
        for s in range(receivers):
            pltpu.make_async_copy(new, out.at[s], out_sems.at[s]).start()
        for s in range(receivers):
            pltpu.make_async_copy(new, out.at[s], out_sems.at[s]).wait()


def wide_layer(me, x, gain, w, receivers):
    count, rows, width = x.shape
    full, cols = w.shape
    chunks = 4
    dma = pltpu.SemaphoreType.DMA
    out_shape = [jax.ShapeDtypeStruct((rows, cols), x.dtype)]
    out_specs = [vmem()]
    scratch = [pltpu.VMEM(x.shape, x.dtype), pltpu.VMEM(w.shape, w.dtype), dma((chunks,)), dma((chunks,))]
    if receivers:
        out_shape.append(jax.ShapeDtypeStruct((receivers, rows, cols), x.dtype))
        out_specs.append(pl.BlockSpec(memory_space=pltpu.HBM))
        scratch.append(dma((receivers,)))

    def kernel(*refs):
        wide_kernel(*refs, receivers=receivers)

    return pl.pallas_call(
        kernel,
        out_shape=out_shape,
        in_specs=[smem(), hbm(), vmem(), hbm()],
        out_specs=out_specs,
        scratch_shapes=scratch,
        compiler_params=params(24),
        name="wide_layer",
    )(me, x, gain, w)


def fetch(parts, shape, use):
    def kernel(*refs):
        out, sems = refs[-2:]
        copies = [
            pltpu.make_async_copy(
                refs[i], out.at[parts[i][1], pl.ds(parts[i][2], parts[i][0].shape[0])], sems.at[n]
            )
            for n, i in enumerate(use)
        ]
        for copy in copies:
            copy.start()
        for copy in copies:
            copy.wait()

    return pl.pallas_call(
        kernel,
        out_shape=jax.ShapeDtypeStruct(shape, jnp.bfloat16),
        in_specs=[hbm()] * len(parts),
        out_specs=vmem(),
        scratch_shapes=[pltpu.SemaphoreType.DMA((len(use),))],
        compiler_params=params(24),
        cost_estimate=pl.CostEstimate(
            flops=0, bytes_accessed=shape[0] * shape[1] * shape[2] * 2, transcendentals=0
        ),
        name="fetch_weights",
    )(*[part for part, _, _ in parts])


def group_kernel(table, *refs, pieces, near, spots):
    got, refs = refs[:pieces], refs[pieces:]
    gain, refs = refs[0], refs[1:]
    copies = []
    if spots:
        sources, refs = refs[: len(spots)], refs[len(spots) :]
        w, sems, refs = refs[-2], refs[-1], refs[:-2]
        copies = [
            pltpu.make_async_copy(
                source, w.at[slot, pl.ds(row, source.shape[0])], sems.at[n]
            )
            for n, (source, (slot, row)) in enumerate(zip(sources, spots))
        ]
        for copy in copies:
            copy.start()
    else:
        w, refs = refs[0], refs[1:]
    new, refs = refs[0], refs[1:]
    x = refs[-1]
    count, rows, width = x.shape
    if pieces == 1:
        x = got[0]
        for j in range(near):
            refs[0][j] = x[table[j]]
    else:
        for k in range(pieces):
            for j in range(near):
                x[table[k * near + j]] = got[k][j]
    squares = jnp.zeros((rows, width), jnp.float32)
    scaled = []
    for s in range(count):
        v = x[s].astype(jnp.float32)
        squares = squares + v * v
        scaled.append((v * gain[s : s + 1, :].astype(jnp.float32)).astype(jnp.bfloat16))
    scaled = jnp.concatenate(scaled, axis=1)
    inv = lax.rsqrt(jnp.sum(squares, axis=1, keepdims=True) / (count * width) + EPSILON)
    for j in range(near):
        for copy, (slot, _) in zip(copies, spots):
            if slot == j:
                copy.wait()
        total = jnp.dot(scaled, w[j], preferred_element_type=jnp.float32)
        new[j] = (x[table[j]].astype(jnp.float32) + inv * total).astype(jnp.bfloat16)


def group_layer(table, got, gain, w=None, parts=(), shape=None):
    near, full, cols = w.shape if shape is None else shape
    rows, width = got[0].shape[1:]
    count = full // width
    piece = jax.ShapeDtypeStruct((near, rows, cols), jnp.bfloat16)
    outs = 2 if len(got) == 1 else 1

    def kernel(*refs):
        group_kernel(
            *refs, pieces=len(got), near=near, spots=[(slot, row) for _, slot, row in parts]
        )

    scratch = [pltpu.VMEM((count, rows, width), jnp.bfloat16)]
    if parts:
        scratch += [pltpu.VMEM(shape, jnp.bfloat16), pltpu.SemaphoreType.DMA((len(parts),))]
        held, specs = [part for part, _, _ in parts], [hbm()] * len(parts)
    else:
        held, specs = [w], [vmem()]
    return pl.pallas_call(
        kernel,
        out_shape=[piece] * outs,
        in_specs=[smem()] + [vmem()] * (len(got) + 1) + specs,
        out_specs=[vmem()] * outs,
        scratch_shapes=scratch,
        compiler_params=params(24),
        name="group_layer",
    )(table, *got, gain, *held)


def unset(*shapes):
    def kernel(*refs):
        pass

    return tuple(
        pl.pallas_call(
            kernel,
            out_shape=[jax.ShapeDtypeStruct(s, jnp.bfloat16) for s in shapes],
            out_specs=[hbm() for _ in shapes],
            name="unset",
        )()
    )


def prune_kernel(weights, keep, out):
    for i in range(keep.shape[0]):
        span = slice(i * BLOCK, (i + 1) * BLOCK)
        out[span, :] = weights[span, :] * (1 - keep[i : i + 1, :]).astype(jnp.bfloat16)


def prune(weights, keep):
    return pl.pallas_call(
        prune_kernel,
        out_shape=jax.ShapeDtypeStruct(weights.shape, weights.dtype),
        in_specs=[vmem()] * 2,
        out_specs=vmem(),
        compiler_params=params(12),
        cost_estimate=pl.CostEstimate(
            flops=weights.size, bytes_accessed=weights.size * 4, transcendentals=0
        ),
        name="prune",
    )(weights, keep)


def set_rows(where, x, size, y, s):
    return x[where[0, y, s], pl.ds(pl.multiple_of(where[1, y, s], size), size), :].astype(jnp.float32)


def error_kernel(where, x, gain, pruned_hbm, error_bf, loss, scaled, pruned, sem):
    fetch_pruned = pltpu.make_async_copy(pruned_hbm, pruned, sem)
    fetch_pruned.start()
    count, rows, width = x.shape
    sets = where.shape[1]
    size = rows // sets
    factors = []
    for y in range(sets):
        squares = jnp.zeros((size, width), jnp.float32)
        for s in range(count):
            v = set_rows(where, x, size, y, s)
            squares = squares + v * v
            scaled[y * size : (y + 1) * size, s * width : (s + 1) * width] = (
                v * gain[s : s + 1, :].astype(jnp.float32)
            ).astype(jnp.bfloat16)
        mean = jnp.sum(squares, axis=1, keepdims=True) / (count * width)
        factors.append(lax.rsqrt(mean + EPSILON))
    inv = jnp.concatenate(factors, axis=0)
    fetch_pruned.wait()
    error = -inv * jnp.dot(scaled[...], pruned[...], preferred_element_type=jnp.float32)
    rounded = error.astype(jnp.bfloat16).astype(jnp.float32)
    error_bf[...] = (rounded * inv).astype(jnp.bfloat16)
    part = jnp.sum(error * error, axis=0, keepdims=True)
    part = part[:, :128] + part[:, 128:]
    loss[...] = jnp.broadcast_to(part, loss.shape)


def layer_error(where, x, gain, pruned):
    count, rows, width = x.shape
    cols = pruned.shape[1]
    return pl.pallas_call(
        error_kernel,
        out_shape=[
            jax.ShapeDtypeStruct((rows, cols), jnp.bfloat16),
            jax.ShapeDtypeStruct((16, 8, 128), jnp.float32),
        ],
        in_specs=[smem()] + [vmem()] * 2 + [hbm()],
        out_specs=[vmem()] * 2,
        scratch_shapes=[
            pltpu.VMEM((rows, count * width), jnp.bfloat16),
            pltpu.VMEM(pruned.shape, pruned.dtype),
            pltpu.SemaphoreType.DMA,
        ],
        compiler_params=params(16),
        name="layer_error",
    )(where, x, gain, pruned)


def grad_kernel(where, x, gain, error_bf, keep, out, *, step, micro_rows):
    count, rows, width = x.shape
    sets = where.shape[1]
    size = rows // sets
    per = width // BLOCK
    first = pl.program_id(0) * step
    for n in range(step):
        s = first + n
        g = gain[pl.ds(s, 1), :].astype(jnp.float32)
        scaled = jnp.concatenate(
            [(set_rows(where, x, size, y, s) * g).astype(jnp.bfloat16) for y in range(sets)], axis=0
        )
        product = lax.dot_general(
            scaled, error_bf[...], (((0,), (0,)), ((), ())), preferred_element_type=jnp.float32
        )
        for b in range(per):
            out[n * width + b * BLOCK : n * width + (b + 1) * BLOCK, :] = (
                product[b * BLOCK : (b + 1) * BLOCK, :]
                * (1.0 / micro_rows)
                * keep[pl.ds(s * per + b, 1), :]
            )


def layer_grad(where, x, gain, error_bf, keep, micro_rows):
    count, rows, width = x.shape
    cols = error_bf.shape[1]
    step = 4

    def kernel(*refs):
        grad_kernel(*refs, step=step, micro_rows=micro_rows)

    return pl.pallas_call(
        kernel,
        grid=(count // step,),
        out_shape=jax.ShapeDtypeStruct((count * width, cols), jnp.float32),
        in_specs=[smem()] + [vmem()] * 4,
        out_specs=pl.BlockSpec((step * width, cols), lambda s: (s, 0)),
        compiler_params=params(16),
        name="layer_grad",
    )(where, x, gain, error_bf, keep)


def shards(layer_input, weight, gain, block_mask):
    layers = lax.axis_size("layer")
    tensors = lax.axis_size("tensor")
    planes = layers // 2
    layer = lax.axis_index("layer")
    me = lax.axis_index("tensor").astype(jnp.int32)
    plane, core = layer // 2, layer % 2
    odd = core == 1
    my_x, my_y = me % SIDE, me // SIDE
    micro, micro_rows, width = layer_input.shape
    rows = micro * micro_rows
    weights = weight[0]
    full_width = weights.shape[0]
    group_rows = rows // SIDE
    piece = (SIDE, group_rows, width)
    half = full_width // 2

    def from_chip(value, shift):
        route = []
        for l in range(layers):
            for t in range(tensors):
                source = ((t // SIDE + shift[1]) % SIDE) * SIDE + (t % SIDE + shift[0]) % SIDE
                route.append((l * tensors + source, l * tensors + t))
        return lax.ppermute(value, AXES, route)

    def swap(value):
        route = [
            (l * tensors + t, (l ^ 1) * tensors + t) for l in range(layers) for t in range(tensors)
        ]
        return lax.ppermute(value, AXES, route)

    def hop(value, to, core=1):
        route = [
            ((2 * to - 1) * tensors + t, (2 * to + core) * tensors + t) for t in range(tensors)
        ]
        return lax.ppermute(value, AXES, route)

    def to_all(value):
        return lax.all_to_all(jnp.broadcast_to(value, (tensors,) + value.shape), "tensor", 0, 0)

    table = jnp.stack(
        [((my_y + j[1]) % SIDE) * SIDE + (my_x + k[0]) % SIDE for k in GROUP for j in NEAR]
    )
    here = me.reshape(1)
    own_gain = gain[0].reshape(tensors, width)

    other_gain = swap(own_gain)
    other_weights = swap(weights)
    held = (SIDE, full_width, width)
    part_shapes = [(half, width)] * 6
    gathered = (tensors, group_rows, width)

    def wide_plane(own):
        x = to_all(own)
        (middle,) = wide_layer(here, x, other_gain, other_weights, 0)
        (new,) = wide_layer(here, to_all(middle), own_gain, weights, 0)
        send = jnp.repeat(new.reshape(piece), SIDE, axis=0)
        return lax.all_to_all(send, "tensor", 0, 0), middle.reshape(piece)

    def first_plane():
        state = lax.cond(
            odd,
            lambda: wide_plane(layer_input.reshape(rows, width)),
            lambda: unset(gathered, piece),
        )
        return state + unset(*part_shapes, *part_shapes)

    def collect_weights():
        low, high = weights[:half], weights[half:]
        up_low, down_high = from_chip(low, (0, 1)), from_chip(high, (0, 3))
        up_high, down_low = from_chip(high, (0, 1)), from_chip(low, (0, 3))
        far_low, far_high = from_chip(up_low, (0, 1)), from_chip(down_high, (0, 3))
        mine = (up_low, up_high, down_low, down_high, far_low, far_high)
        return unset(gathered, piece) + mine + tuple(swap(part) for part in mine)

    new, middle, *parts = lax.cond(plane < 1, first_plane, collect_weights)
    before = middle
    spots = [(0, 0)] + [(slot, row) for slot in (1, 2, 3) for row in (0, half)]
    sources = [weights] + parts[:6] + [other_weights] + parts[6:]
    parts = [(source,) + spots[i % 7] for i, source in enumerate(sources)]
    mine, other = tuple(range(7)), tuple(range(7, 14))

    def exchange(own):
        return [own] + [from_chip(own, k) for k in GROUP[1:]]

    def group_plane(step, own):
        if step == 1:
            middle, own = group_layer(
                table, [own], other_gain, parts=[parts[i] for i in other], shape=held
            )
        else:
            got = exchange(own)
            w = fetch(parts, held, other)
            (middle,) = group_layer(table, got, other_gain, w)
        if step == planes - 1:
            return middle
        w = fetch(parts, held, mine)
        (new,) = group_layer(table, exchange(middle), own_gain, w)
        return new, own, middle

    for step in range(1, planes - 1):
        came = hop(new, step)
        skipped = unset(piece)[0] if step == 1 else came
        if step == planes - 2:
            came, again = lax.optimization_barrier((came, new))
            before_last = hop(again, step, 0)
        new, before, middle = lax.cond(
            (plane == step) & odd,
            lambda came=came, step=step: group_plane(step, came),
            lambda new=skipped, a=before, b=middle: (new, a, b),
        )
    came = hop(new, planes - 1)
    came, again = lax.optimization_barrier((came, new))
    for_even = hop(again, planes - 1, 0)

    def piece_of_plane():
        even = lax.cond(plane == planes - 2, lambda: before_last, lambda: swap(before))
        return jnp.where(odd, middle, jnp.where(plane == 0, layer_input.reshape(piece), even))

    own_piece = lax.cond(
        plane == planes - 1,
        lambda: lax.cond(odd, lambda: group_plane(planes - 1, came), lambda: for_even),
        piece_of_plane,
    )
    keep = jnp.repeat(block_mask[0].astype(jnp.float32), BLOCK, axis=1)
    wide_table = np.zeros((2, SIDE, tensors), np.int32)
    group_table = np.zeros((2, SIDE, tensors), np.int32)
    for y in range(SIDE):
        for s in range(tensors):
            wide_table[:, y, s] = s, y * group_rows
            for j, (_, shift) in enumerate(NEAR):
                if (y + shift) % SIDE == s // SIDE:
                    group_table[:, y, s] = y * SIDE + s % SIDE, j * group_rows
    where = jnp.where(plane < 1, jnp.asarray(wide_table), jnp.asarray(group_table))
    full_gain = own_gain.astype(jnp.float32)
    send = jnp.broadcast_to(own_piece, (tensors,) + own_piece.shape)
    send, late_weights = lax.optimization_barrier((send, weights))
    x = lax.all_to_all(send, "tensor", 0, 0).reshape(tensors, rows, width)
    pruned = prune(late_weights, keep)
    error_bf, loss = layer_error(where, x, full_gain, pruned)
    shares = lax.all_to_all(loss, "tensor", 0, 0)
    grad = layer_grad(where, x, full_gain, error_bf, keep, micro_rows)
    total = jnp.sum(shares[:, 0, :]) / (micro_rows * full_width)
    return grad[None], total.reshape(1)


def solution(mesh):
    in_specs = (
        P(None, None, "tensor"),
        P("layer", None, "tensor"),
        P("layer", None),
        P("layer", None, "tensor"),
    )
    out_specs = (P("layer", None, "tensor"), P("layer"))
    return jax.shard_map(shards, mesh=mesh, in_specs=in_specs, out_specs=out_specs, check_vma=False)
```
